128 devices in a mesh: clus: 32 (over z, y, core), row: 4 (over x).
Axes of the slice: x: 4, y: 4, z: 4, core: 2. Of those that a mesh axis runs over, the one named last changes fastest.
Arguments:
- operator: bfloat16 [32, 1024, 32768], P(None, 'row', 'clus'), may hold values from -0.03125 to 0.03125
- omega: bfloat16 [32768, 256], P('clus'), may hold values from -6 to 6
- omega_rows: bfloat16 [32768, 256], P(('clus', 'row')), may hold values from -6 to 6
- near_list: int32 [32, 3], replicated, may hold values from 0 to 31, as said below
Outputs:
- col_basis: float32 [32768, 128], P(('clus', 'row'))
- row_basis: float32 [32768, 128], P(('clus', 'row'))
- col_transfers: float32 [32, 3, 256, 128], P('clus')
- row_transfers: float32 [32, 3, 256, 128], P('clus')
- col_top: float32 [32, 128, 256], P('clus')
- row_top: float32 [32, 128, 256], P('clus')
The draws below stay inside these ranges and needn't reach their ends.
Inputs may be any that keep to these rules, and one draw needn't show every extreme that they name: `near_list`: row t lists 3 different clusters, the first being t itself.
All inputs are finite; a program needn't handle non-finite values.
Results may differ from the reference program's by a relative error of at most 0.0032.
Values may be sent and summed in bfloat16 or wider, within the bound.
A program may use at most 128 MiB of HBM per device.

```python
import math
import jax
import jax.numpy as jnp
from jax import lax

RC = 1024
S = 256
R = 128
NNEAR = 3
MERGES = 3
NCLUS = 32
N = 32768


def draw_near_list(key, part):
    key = jax.random.fold_in(key, 7)
    scores = jax.random.randint(key, (NCLUS, NCLUS), 0, 1 << 20) * NCLUS + jnp.arange(NCLUS, dtype=jnp.int32)[None, :]
    diagonal_mask = jnp.arange(NCLUS)[:, None] == jnp.arange(NCLUS)[None, :]
    scores = jnp.where(diagonal_mask, -1, scores)
    ranked = jnp.argsort(scores, axis=1, stable=True)
    return ranked[:, :NNEAR].astype(jnp.int32)


def levels(own_key, dims, pieces, least, high):
    level, own = 1.0, jax.random.fold_in(own_key, 6)
    for axis_at, blocks in pieces:
        draws = jnp.exp(jax.random.uniform(jax.random.fold_in(own, axis_at), (blocks,), jnp.float32, least / len(pieces), high / len(pieces)))
        level = level * jnp.repeat(draws, dims[axis_at] // blocks).reshape([-1 if axis == axis_at else 1 for axis in range(len(dims))])
    return level


def scatter_about(key, dims, width, limit, split=(), kind=jnp.bfloat16):
    drawn = width * jax.random.normal(key, dims, jnp.float32)
    if split:
        drawn = drawn * levels(key, dims, split, -0.22, 0.18)
    return jnp.clip(drawn, -limit, limit).astype(kind)


def setup_inputs(seed: int = 0) -> dict:
    keys = jax.random.split(jax.random.key(seed), 5)
    operator = scatter_about(keys[0], (NCLUS, RC, N), N ** -0.5, 0.03125, ((1, 4), (2, 32)))
    omega = scatter_about(keys[1], (N, S), 1.0, 6.0, ((0, 32),))
    omega_rows = scatter_about(keys[2], (N, S), 1.0, 6.0, ((0, 128),))
    near_list = draw_near_list(jax.random.fold_in(keys[4], 71), 0)
    return {"operator": operator, "omega": omega, "omega_rows": omega_rows, "near_list": near_list}


HIGHEST = lax.Precision.HIGHEST

def far_table(near_list):
    clusters = jnp.arange(NCLUS, dtype=jnp.int32)
    matched = near_list[:, :, None] == clusters[None, None, :]
    return 1.0 - lax.optimization_barrier(jnp.max(matched.astype(jnp.float32), axis=1))

def factor(leading, stacked):
    gram_rows = lax.dot_general(leading.astype(jnp.float32), stacked.astype(jnp.float32), (((0,), (0,)), ((), ())), precision=HIGHEST, preferred_element_type=jnp.float32)
    factor_low = jnp.linalg.cholesky(gram_rows[:, :R])
    basis_part = lax.linalg.triangular_solve(factor_low, leading, left_side=False, lower=True, transpose_a=True)
    coeffs = lax.linalg.triangular_solve(factor_low, gram_rows, left_side=True, lower=True)
    return (basis_part, coeffs)

def factor_whole(stacked):
    return factor(stacked[:, :R], stacked)

def tree_merge(leaf_coeffs):
    current = leaf_coeffs
    transfers = []
    for level_no in range(MERGES):
        groups = current.shape[0] // 2
        stacked = current.reshape(groups, 2 * R, S)
        moved, current = jax.vmap(factor_whole)(stacked)
        transfers.append(jnp.repeat(moved, 2 ** (level_no + 1), axis=0))
    top_level = jnp.repeat(current, 2 ** MERGES, axis=0)
    return (jnp.stack(transfers, axis=1) * math.sqrt(2 * R), top_level / math.sqrt(RC))

def reference(operator, omega, omega_rows, near_list):
    far = far_table(near_list)
    panels_rows = omega_rows.reshape(NCLUS, RC, S).astype(jnp.float32)

    def one_column(running, column):
        block_cols = lax.dynamic_slice_in_dim(operator, column * RC, RC, 2).astype(jnp.float32)
        panel_cols = lax.dynamic_slice_in_dim(omega, column * RC, RC, 0).astype(jnp.float32)
        weights = lax.dynamic_index_in_dim(far, column, 1, keepdims=False)
        product = jnp.einsum('tij,js->tis', block_cols, panel_cols, precision=HIGHEST)
        product = (product * weights[:, None, None]).astype(jnp.bfloat16)
        product = lax.optimization_barrier(product).astype(jnp.float32)
        masked = panels_rows * weights[:, None, None]
        back_sum = jnp.einsum('tij,tis->js', block_cols, masked, precision=HIGHEST)
        return (running + product, back_sum)
    start_value = jnp.zeros((NCLUS, RC, S), jnp.float32)
    col_sample, row_sample = lax.scan(one_column, start_value, jnp.arange(NCLUS, dtype=jnp.int32))
    col_leaf, col_coeffs = jax.vmap(factor_whole)(col_sample)
    row_leaf, row_coeffs = jax.vmap(factor_whole)(row_sample)
    col_transfers, col_top = tree_merge(col_coeffs)
    row_transfers, row_top = tree_merge(row_coeffs)
    scale = math.sqrt(RC)
    col_basis = col_leaf.reshape(N, R) * scale
    row_basis = row_leaf.reshape(N, R) * scale
    return (col_basis, row_basis, col_transfers, row_transfers, col_top, row_top)
```

```python
import math

import jax
import jax.numpy as jnp
from jax import lax
from jax.experimental import pallas as pl
from jax.experimental.pallas import tpu as pltpu
from jax.sharding import PartitionSpec as P

R = 128
F32 = jnp.float32
MERGES = 3


HIGHEST = lax.Precision.HIGHEST


def partner(x, axis, apart):
    return lax.ppermute(x, axis, [(i, i ^ 1 << apart) for i in range(lax.axis_size(axis))])


def far_table(near_list, cluster_count):
    clusters = jnp.arange(cluster_count, dtype=jnp.int32)
    matched = near_list[:, :, None] == clusters[None, None, :]
    return 1.0 - jnp.max(matched.astype(jnp.float32), axis=1)


def local_gram(leading, stacked):
    return lax.dot_general(
        leading,
        stacked,
        (((0,), (0,)), ((), ())),
        precision=HIGHEST,
        preferred_element_type=jnp.float32,
    )


def split3(x):
    hi = x.astype(jnp.bfloat16).astype(F32)
    rest = x - hi
    mid = rest.astype(jnp.bfloat16).astype(F32)
    low = rest - mid
    return hi, mid, low

def panel(state, m, first):
    rows = state[m, first:first + 8, :]
    place = lax.broadcasted_iota(jnp.int32, (8, R), 0)
    place2 = lax.broadcasted_iota(jnp.int32, (8, 2 * R), 0)
    cols = [jnp.broadcast_to(rows[:, first + c:first + c + 1], (8, R)) for c in range(8)]
    for c in range(8):
        scale = lax.rsqrt(jnp.broadcast_to(cols[c][c:c + 1, :], (8, R)))
        mult = jnp.where(place > c, cols[c] * scale, 0.0)
        for k in range(c + 1, 8):
            cols[k] = cols[k] - mult * (jnp.broadcast_to(cols[k][c:c + 1, :], (8, R)) * scale)
        scale2 = jnp.concatenate([scale, scale], axis=1)
        mult2 = jnp.concatenate([mult, mult], axis=1)
        pivot = jnp.broadcast_to(rows[c:c + 1, :], (8, 2 * R)) * scale2
        rows = jnp.where(place2 == c, pivot, rows - mult2 * pivot)
    state[m, first:first + 8, :] = rows
    last = first + 8
    if last < R:
        hi, mid, low = split3(rows)
        left = jnp.concatenate([hi, hi, mid, mid, hi, low], axis=0).astype(jnp.bfloat16)
        right = jnp.concatenate([hi, mid, hi, mid, low, hi], axis=0).astype(jnp.bfloat16)
        state[m, last:, :] -= lax.dot_general(left[:, last:R] if last % R == 0 else left[:, :R], right, (((0,), (0,)), ((), ())), preferred_element_type=F32)[last:, :]

def chol_all(state, count):
    for first in range(0, R, 8):
        for m in range(count):
            panel(state, m, first)

def factor_kernel(bits_ref, gram_ref, side_ref, sample_ref, basis_ref, trans_ref, top_ref, state):
    eye_rows = lax.broadcasted_iota(jnp.int32, (R, R), 0)
    eye_cols = lax.broadcasted_iota(jnp.int32, (R, R), 1)
    eye = (eye_rows == eye_cols).astype(F32)
    count = gram_ref.shape[0]
    for m in range(count):
        state[m, :, :R] = gram_ref[m]
        state[m, :, R:] = eye
    chol_all(state, count)
    for m in range(count):
        state[m, :, :R] = jnp.where(eye_cols >= eye_rows, state[m, :, :R], 0.0)
    half = count // 2
    outer = (((1,), (1,)), ((), ()))
    for s in range(2):
        inverse = state[s * half + bits_ref[0], :, R:]
        basis_ref[s] = lax.dot_general(
            sample_ref[s], inverse, outer, precision=HIGHEST, preferred_element_type=F32
        ) * math.sqrt(1024)
        for k in range(MERGES):
            at = 2 * (k + 1) + (bits_ref[k + 1] if k + 1 < MERGES else 0)
            inverse = state[s * half + at, :, R:] * math.sqrt(2 * R)
            for h in range(2):
                trans_ref[s, k, h * R:(h + 1) * R, :] = lax.dot_general(
                    state[s * half + 2 * k + h, :, :R],
                    inverse,
                    outer,
                    precision=HIGHEST,
                    preferred_element_type=F32,
                )
        last = s * half + 2 * MERGES
        top_ref[s, :, :R] = state[last, :, :R] * (1.0 / math.sqrt(1024))
        top_ref[s, :, R:] = jnp.dot(
            state[last, :, R:], side_ref[s], precision=HIGHEST, preferred_element_type=F32
        ) * (1.0 / math.sqrt(1024))


def factor_all(bits, grams, side, samples):
    vmem = pl.BlockSpec(memory_space=pltpu.VMEM)
    count, rows = grams.shape[0], samples.shape[1]
    return pl.pallas_call(
        factor_kernel,
        out_shape=[
            jax.ShapeDtypeStruct((2, rows, R), F32),
            jax.ShapeDtypeStruct((2, MERGES, 2 * R, R), F32),
            jax.ShapeDtypeStruct((2, R, 2 * R), F32),
        ],
        in_specs=[pl.BlockSpec(memory_space=pltpu.SMEM), vmem, vmem, vmem],
        out_specs=[vmem, vmem, vmem],
        scratch_shapes=[pltpu.VMEM((count, R, 2 * R), F32)],
        compiler_params=pltpu.CompilerParams(vmem_limit_bytes=40 << 20),
    )(bits, grams, side, samples)


def body(operator, omega, omega_rows, near_list):
    cluster_count = operator.shape[0]
    rows_share = operator.shape[1]
    width = operator.shape[2]
    my_index = lax.axis_index("clus")
    far = far_table(near_list, cluster_count)
    far_mine = lax.dynamic_index_in_dim(far, my_index, 1, keepdims=False)
    products = jnp.einsum("tij,js->tis", operator, omega, preferred_element_type=jnp.float32)
    products = (products * far_mine[:, None, None]).astype(jnp.bfloat16)
    received = lax.all_to_all(products, "clus", split_axis=0, concat_axis=0, tiled=True)
    operator_rows = operator.reshape(cluster_count * rows_share, width)
    block_part = lax.all_gather(omega_rows, "clus", axis=0, tiled=True)
    piece_rows = block_part.shape[0]
    owners = lax.iota(jnp.int32, piece_rows) // rows_share
    one_hot = (owners[:, None] == lax.iota(jnp.int32, cluster_count)[None, :]).astype(jnp.float32)
    weights = jnp.dot(one_hot, far_mine, precision=HIGHEST)
    scaled = block_part * weights.astype(jnp.bfloat16)[:, None]
    partial_sum = lax.dot_general(
        operator_rows, scaled, (((0,), (0,)), ((), ())), preferred_element_type=jnp.float32
    )
    sample_u = jnp.sum(received.astype(jnp.float32), axis=0)
    leading_u = sample_u[:, :R]
    gram_u_local = local_gram(leading_u, sample_u)
    share_v = lax.psum_scatter(partial_sum, "row", scatter_dimension=0, tiled=True)
    gram_v_local = local_gram(share_v[:, :R], share_v)
    gram_u, gram_v = lax.psum((gram_u_local, gram_v_local), "row")
    total = jnp.stack([gram_u, gram_v])
    ordered = []
    for level_no in range(MERGES):
        sibling = partner(total, "clus", level_no)
        on_left = my_index >> level_no & 1 == 0
        ordered.append(jnp.where(on_left, total, sibling)[:, :, :R])
        ordered.append(jnp.where(on_left, sibling, total)[:, :, :R])
        total = total + sibling
    ordered.append(total[:, :, :R])
    grams = jnp.stack(ordered, axis=1).reshape(2 * (2 * MERGES + 1), R, R)
    bits = (my_index >> jnp.arange(4, dtype=jnp.int32)) & 1
    samples = jnp.stack([leading_u, share_v[:, :R]])
    basis, trans, top = factor_all(bits, grams, total[:, :, R:], samples)
    return (basis[0], basis[1], trans[0][None], trans[1][None], top[0][None], top[1][None])


def solution(mesh):
    in_specs = (P(None, "row", "clus"), P("clus", None), P(("clus", "row"), None), P())
    out_specs = (
        P(("clus", "row"), None),
        P(("clus", "row"), None),
        P("clus", None, None, None),
        P("clus", None, None, None),
        P("clus", None, None),
        P("clus", None, None),
    )
    return jax.shard_map(body, mesh=mesh, in_specs=in_specs, out_specs=out_specs, check_vma=False)
```

```python
import math

import jax
import jax.numpy as jnp
from jax import lax
from jax.experimental import pallas as pl
from jax.experimental.pallas import tpu as pltpu
from jax.sharding import PartitionSpec as P

R = 128
F32 = jnp.float32
MERGES = 3


HIGHEST = lax.Precision.HIGHEST


def partner(x, axis, apart):
    return lax.ppermute(x, axis, [(i, i ^ 1 << apart) for i in range(lax.axis_size(axis))])


def far_table(near_list, cluster_count):
    clusters = jnp.arange(cluster_count, dtype=jnp.int32)
    matched = near_list[:, :, None] == clusters[None, None, :]
    return 1.0 - jnp.max(matched.astype(jnp.float32), axis=1)


def local_gram(leading, stacked):
    return lax.dot_general(
        leading,
        stacked,
        (((0,), (0,)), ((), ())),
        precision=HIGHEST,
        preferred_element_type=jnp.float32,
    )


def split3(x):
    hi = x.astype(jnp.bfloat16).astype(F32)
    rest = x - hi
    mid = rest.astype(jnp.bfloat16).astype(F32)
    low = rest - mid
    return hi, mid, low

def panel(state, m, first):
    rows = state[m, first:first + 8, :]
    place = lax.broadcasted_iota(jnp.int32, (8, R), 0)
    place2 = lax.broadcasted_iota(jnp.int32, (8, 2 * R), 0)
    cols = [jnp.broadcast_to(rows[:, first + c:first + c + 1], (8, R)) for c in range(8)]
    for c in range(8):
        scale = lax.rsqrt(jnp.broadcast_to(cols[c][c:c + 1, :], (8, R)))
        mult = jnp.where(place > c, cols[c] * scale, 0.0)
        for k in range(c + 1, 8):
            cols[k] = cols[k] - mult * (jnp.broadcast_to(cols[k][c:c + 1, :], (8, R)) * scale)
        scale2 = jnp.concatenate([scale, scale], axis=1)
        mult2 = jnp.concatenate([mult, mult], axis=1)
        pivot = jnp.broadcast_to(rows[c:c + 1, :], (8, 2 * R)) * scale2
        rows = jnp.where(place2 == c, pivot, rows - mult2 * pivot)
    state[m, first:first + 8, :] = rows
    last = first + 8
    if last < R:
        hi, mid, low = split3(rows)
        left = jnp.concatenate([hi, hi, mid, mid, hi, low], axis=0).astype(jnp.bfloat16)
        right = jnp.concatenate([hi, mid, hi, mid, low, hi], axis=0).astype(jnp.bfloat16)
        state[m, last:, :] -= lax.dot_general(left[:, last:R] if last % R == 0 else left[:, :R], right, (((0,), (0,)), ((), ())), preferred_element_type=F32)[last:, :]

def chol_all(state, count):
    for first in range(0, R, 8):
        for m in range(count):
            panel(state, m, first)

def factor_kernel(bits_ref, gram_ref, side_ref, sample_ref, basis_ref, trans_ref, top_ref, state):
    eye_rows = lax.broadcasted_iota(jnp.int32, (R, R), 0)
    eye_cols = lax.broadcasted_iota(jnp.int32, (R, R), 1)
    eye = (eye_rows == eye_cols).astype(F32)
    count = gram_ref.shape[0]
    for m in range(count):
        state[m, :, :R] = gram_ref[m]
        state[m, :, R:] = eye
    chol_all(state, count)
    for m in range(count):
        state[m, :, :R] = jnp.where(eye_cols >= eye_rows, state[m, :, :R], 0.0)
    half = count // 2
    outer = (((1,), (1,)), ((), ()))
    for s in range(2):
        inverse = state[s * half + bits_ref[0], :, R:]
        basis_ref[s] = lax.dot_general(
            sample_ref[s], inverse, outer, precision=HIGHEST, preferred_element_type=F32
        ) * math.sqrt(1024)
        for k in range(MERGES):
            at = 2 * (k + 1) + (bits_ref[k + 1] if k + 1 < MERGES else 0)
            inverse = state[s * half + at, :, R:] * math.sqrt(2 * R)
            for h in range(2):
                trans_ref[s, k, h * R:(h + 1) * R, :] = lax.dot_general(
                    state[s * half + 2 * k + h, :, :R],
                    inverse,
                    outer,
                    precision=HIGHEST,
                    preferred_element_type=F32,
                )
        last = s * half + 2 * MERGES
        top_ref[s, :, :R] = state[last, :, :R] * (1.0 / math.sqrt(1024))
        top_ref[s, :, R:] = jnp.dot(
            state[last, :, R:], side_ref[s], precision=HIGHEST, preferred_element_type=F32
        ) * (1.0 / math.sqrt(1024))


def factor_all(bits, grams, side, samples):
    vmem = pl.BlockSpec(memory_space=pltpu.VMEM)
    count, rows = grams.shape[0], samples.shape[1]
    return pl.pallas_call(
        factor_kernel,
        out_shape=[
            jax.ShapeDtypeStruct((2, rows, R), F32),
            jax.ShapeDtypeStruct((2, MERGES, 2 * R, R), F32),
            jax.ShapeDtypeStruct((2, R, 2 * R), F32),
        ],
        in_specs=[pl.BlockSpec(memory_space=pltpu.SMEM), vmem, vmem, vmem],
        out_specs=[vmem, vmem, vmem],
        scratch_shapes=[pltpu.VMEM((count, R, 2 * R), F32)],
        compiler_params=pltpu.CompilerParams(vmem_limit_bytes=40 << 20),
    )(bits, grams, side, samples)


SIDE = 4
MESH = pl.DeviceIdType.MESH


def place_of():
    clus = lax.axis_index("clus")
    return (clus // 8, clus // 2 % SIDE, clus % 2)


def clus_at(z, y, core):
    return {"clus": (z % SIDE * SIDE + y % SIDE) * 2 + core}


def remote(src, dst, send, recv, device):
    return pltpu.make_async_remote_copy(
        src_ref=src, dst_ref=dst, send_sem=send, recv_sem=recv, device_id=device, device_id_type=MESH
    )


def meet(devices):
    barrier = pltpu.get_barrier_semaphore()
    for device in devices:
        pl.semaphore_signal(barrier, inc=1, device_id=device, device_id_type=MESH)
    pl.semaphore_wait(barrier, len(devices))


def sample_kernel(
    far, op_hbm, omega, q_own, u_out, v_out,
    op, own, away, fromcore, zin, yin, zpart, ypart, zlast, ylast, gathered, total, vsend, vin,
    op_sem, ag_send, ag_recv, fw_send, fw_recv, core_send, core_recv,
    rs_send, rs_recv, last_send, last_recv, v_send, v_recv,
):
    z, y, core = place_of()
    x = lax.axis_index("row")
    here = z * SIDE + y
    other = 1 - core
    half = (pl.ds(0, 128), pl.ds(128, 128))
    steps = (1, 2, 3)

    def load(t):
        return pltpu.make_async_copy(op_hbm.at[t], op.at[t], op_sem.at[t])

    def spot(a, b):
        return (z - a + SIDE) % SIDE * SIDE + (y - b + SIDE) % SIDE

    def gather_send(h, a, b, along):
        piece = gathered.at[core, spot(a, b), half[h]]
        if h == 0:
            return remote(piece, piece, ag_send.at[h, along, b], ag_recv.at[h, along, b], clus_at(z + along, y, core))
        return remote(piece, piece, ag_send.at[h, a, along], ag_recv.at[h, a, along], clus_at(z, y + along, core))

    def gather_first(h, along):
        piece = gathered.at[core, here, half[h]]
        if h == 0:
            return remote(piece, piece, ag_send.at[h, 0, along], ag_recv.at[h, 0, along], clus_at(z, y + along, core))
        return remote(piece, piece, ag_send.at[h, along, 0], ag_recv.at[h, along, 0], clus_at(z + along, y, core))

    def arrived(h, a, b):
        piece = gathered.at[core, spot(a, b), half[h]]
        return remote(piece, piece, ag_send.at[h, a, b], ag_recv.at[h, a, b], clus_at(z, y, other))

    def forward(which, h, a, b):
        piece = gathered.at[which, spot(a, b), half[h]]
        return remote(piece, piece, fw_send.at[h, a, b], fw_recv.at[h, a, b], clus_at(z, y, other))

    def to_core(i):
        return remote(away.at[i], fromcore.at[i], core_send.at[i], core_recv.at[i], clus_at(z, y, other))

    def scatter(h, a, b):
        zt, yt = (z + a) % SIDE, (y + b) % SIDE
        block = own.at[zt * SIDE + yt, half[h]]
        if h == 0:
            return remote(block, zin.at[a, yt], rs_send.at[h, a, b], rs_recv.at[h, a, b], clus_at(zt, y, core))
        return remote(block, yin.at[b, zt], rs_send.at[h, a, b], rs_recv.at[h, a, b], clus_at(z, yt, core))

    def scatter_last(h, along):
        if h == 0:
            yt = (y + along) % SIDE
            return remote(zpart.at[yt], ylast.at[along], last_send.at[h, along], last_recv.at[h, along], clus_at(z, yt, core))
        zt = (z + along) % SIDE
        return remote(ypart.at[zt], zlast.at[along], last_send.at[h, along], last_recv.at[h, along], clus_at(zt, y, core))

    def row_send(along):
        xt = (x + along) % SIDE
        return remote(vsend.at[xt], vin.at[along], v_send.at[along], v_recv.at[along], {"row": xt})

    def loads(i, _):
        load(2 * i + other).start()
        load(2 * i + core).start()
        return 0

    lax.fori_loop(0, 16, loads, 0)
    meet(
        [clus_at(z, y, other)]
        + [clus_at(z, y + d, core) for d in steps]
        + [clus_at(z + d, y, core) for d in steps]
        + [{"row": (x + d) % SIDE} for d in steps]
    )
    gathered[core, here] = q_own[...].astype(F32).T.astype(jnp.bfloat16)
    for d in (1, 3, 2):
        for h in range(2):
            gather_first(h, d).start()
    for d in (1, 3, 2):
        for h in range(2):
            gather_send(h, 0, 0, d).start()
    for h in range(2):
        forward(core, h, 0, 0).start()

    def column(i, _):
        for which, keep in ((other, away), (core, own)):
            t = 2 * i + which
            load(t).wait()
            product = jnp.dot(op[t], omega[...], preferred_element_type=F32) * far[t]
            keep[i] = product.astype(jnp.bfloat16)
            if keep is away:
                to_core(i).start()
        return 0

    lax.fori_loop(0, 8, column, 0)
    for d in (1, 3, 2):
        for h, a, b in ((0, 0, d), (1, d, 0)):
            arrived(h, a, b).wait_recv()
            for along in (1, 3, 2):
                gather_send(h, a, b, along).start()
            forward(core, h, a, b).start()
    lax.fori_loop(8, 16, column, 0)

    def pair_sum(i, _):
        a, b = i // SIDE, i % SIDE
        at = (z + a) % SIDE * SIDE + (y + b) % SIDE
        to_core(at).wait_recv()
        own[at] = (own[at].astype(F32) + fromcore[at].astype(F32)).astype(jnp.bfloat16)

        @pl.when(a != 0)
        def _():
            scatter(0, a, b).start()

        @pl.when(b != 0)
        def _():
            scatter(1, a, b).start()

        return 0

    lax.fori_loop(0, 16, pair_sum, 0)
    total[...] = jnp.zeros_like(total)

    def row_step(which, at):
        t = 2 * at + which
        piece = (gathered[which, at].astype(F32) * far[t]).astype(jnp.bfloat16)
        total[...] += jnp.dot(piece, op[t], preferred_element_type=F32)

    def row_own(i, _):
        a, b = i // SIDE, i % SIDE

        @pl.when(a != 0)
        def _():
            arrived(0, a, b).wait_recv()
            forward(core, 0, a, b).start()

        @pl.when(b != 0)
        def _():
            arrived(1, a, b).wait_recv()
            forward(core, 1, a, b).start()

        row_step(core, spot(a, b))
        return 0

    lax.fori_loop(0, 16, row_own, 0)

    def row_other(i, _):
        a, b = i // SIDE, i % SIDE
        for h in range(2):
            forward(other, h, a, b).wait_recv()
        row_step(other, spot(a, b))
        return 0

    lax.fori_loop(0, 16, row_other, 0)
    for quarter in range(SIDE):
        vsend[quarter] = total[:, quarter * 256:(quarter + 1) * 256].astype(jnp.bfloat16)
    for d in (1, 3, 2):
        row_send(d).start()

    def first_sum(i, _):
        yt = (y + i) % SIDE
        for d in steps:
            scatter(0, d, i).wait_recv()
        part = own[z * SIDE + yt, half[0]].astype(F32)
        for d in steps:
            part = part + zin[d, yt].astype(F32)
        zpart[yt] = part.astype(jnp.bfloat16)

        @pl.when(i == 0)
        def _():
            u_out[half[0], :] = part

        zt = (z + i) % SIDE
        for d in steps:
            scatter(1, i, d).wait_recv()
        part = own[zt * SIDE + y, half[1]].astype(F32)
        for d in steps:
            part = part + yin[d, zt].astype(F32)
        ypart[zt] = part.astype(jnp.bfloat16)

        @pl.when(i == 0)
        def _():
            u_out[half[1], :] = part

        @pl.when(i != 0)
        def _():
            scatter_last(0, i).start()
            scatter_last(1, i).start()

        return 0

    lax.fori_loop(0, SIDE, first_sum, 0)
    for d in steps:
        row_send(d).wait_recv()
    share = total[:, pl.ds(pl.multiple_of(x * 256, 256), 256)]
    for d in steps:
        share = share + vin[d].astype(F32)
    v_out[...] = share.T
    for h in range(2):
        late = (ylast, zlast)[h]
        for d in steps:
            scatter_last(h, d).wait_recv()
        part = u_out[half[h], :]
        for d in steps:
            part = part + late[d].astype(F32)
        u_out[half[h], :] = part

    for d in steps:
        row_send(d).wait_send()
        for h in range(2):
            gather_first(h, d).wait_send()
            scatter_last(h, d).wait_send()

    def drain(i, _):
        a, b = i // SIDE, i % SIDE
        to_core(i).wait_send()
        for h in range(2):
            forward(core, h, a, b).wait_send()

        @pl.when(a != 0)
        def _():
            arrived(0, a, b).wait_send()
            scatter(0, a, b).wait_send()

        @pl.when(b != 0)
        def _():
            arrived(1, a, b).wait_send()
            scatter(1, a, b).wait_send()

        return 0

    lax.fori_loop(0, 16, drain, 0)


def samples_of(far, operator, omega, omega_rows):
    vmem = pl.BlockSpec(memory_space=pltpu.VMEM)
    bf16 = jnp.bfloat16
    sem = pltpu.SemaphoreType.DMA
    block = (256, 256)
    part = (128, 256)
    return pl.pallas_call(
        sample_kernel,
        out_shape=[jax.ShapeDtypeStruct(block, F32)] * 2,
        in_specs=[pl.BlockSpec(memory_space=pltpu.SMEM), pl.BlockSpec(memory_space=pl.ANY), vmem, vmem],
        out_specs=[vmem, vmem],
        scratch_shapes=[
            pltpu.VMEM(operator.shape, bf16),
            pltpu.VMEM((16, *block), bf16),
            pltpu.VMEM((16, *block), bf16),
            pltpu.VMEM((16, *block), bf16),
            pltpu.VMEM((SIDE, SIDE, *part), bf16),
            pltpu.VMEM((SIDE, SIDE, *part), bf16),
            pltpu.VMEM((SIDE, *part), bf16),
            pltpu.VMEM((SIDE, *part), bf16),
            pltpu.VMEM((SIDE, *part), bf16),
            pltpu.VMEM((SIDE, *part), bf16),
            pltpu.VMEM((2, 16, *block), bf16),
            pltpu.VMEM((256, 1024), F32),
            pltpu.VMEM((SIDE, *block), bf16),
            pltpu.VMEM((SIDE, *block), bf16),
            sem((32,)),
            sem((2, SIDE, SIDE)),
            sem((2, SIDE, SIDE)),
            sem((2, SIDE, SIDE)),
            sem((2, SIDE, SIDE)),
            sem((16,)),
            sem((16,)),
            sem((2, SIDE, SIDE)),
            sem((2, SIDE, SIDE)),
            sem((2, SIDE)),
            sem((2, SIDE)),
            sem((SIDE,)),
            sem((SIDE,)),
        ],
        compiler_params=pltpu.CompilerParams(
            collective_id=0, has_side_effects=True, vmem_limit_bytes=48 << 20
        ),
        cost_estimate=pl.CostEstimate(flops=1 << 33, bytes_accessed=1 << 24, transcendentals=0),
    )(far, operator, omega, omega_rows)


def body(operator, omega, omega_rows, near_list):
    my_index = lax.axis_index("clus")
    far = far_table(near_list, operator.shape[0])
    far_mine = lax.dynamic_index_in_dim(far, my_index, 1, keepdims=False)
    sample_u, share_v = samples_of(far_mine, operator, omega, omega_rows)
    leading_u = sample_u[:, :R]
    gram_u_local = local_gram(leading_u, sample_u)
    gram_v_local = local_gram(share_v[:, :R], share_v)
    gram_u, gram_v = lax.psum((gram_u_local, gram_v_local), "row")
    total = jnp.stack([gram_u, gram_v])
    ordered = []
    for level_no in range(MERGES):
        sibling = partner(total, "clus", level_no)
        on_left = my_index >> level_no & 1 == 0
        ordered.append(jnp.where(on_left, total, sibling)[:, :, :R])
        ordered.append(jnp.where(on_left, sibling, total)[:, :, :R])
        total = total + sibling
    ordered.append(total[:, :, :R])
    grams = jnp.stack(ordered, axis=1).reshape(2 * (2 * MERGES + 1), R, R)
    bits = (my_index >> jnp.arange(4, dtype=jnp.int32)) & 1
    samples = jnp.stack([leading_u, share_v[:, :R]])
    basis, trans, top = factor_all(bits, grams, total[:, :, R:], samples)
    return (basis[0], basis[1], trans[0][None], trans[1][None], top[0][None], top[1][None])


def solution(mesh):
    in_specs = (P(None, "row", "clus"), P("clus", None), P(("clus", "row"), None), P())
    out_specs = (
        P(("clus", "row"), None),
        P(("clus", "row"), None),
        P("clus", None, None, None),
        P("clus", None, None, None),
        P("clus", None, None),
        P("clus", None, None),
    )
    return jax.shard_map(body, mesh=mesh, in_specs=in_specs, out_specs=out_specs, check_vma=False)
```

```python
import math

import jax
import jax.numpy as jnp
from jax import lax
from jax.experimental import pallas as pl
from jax.experimental.pallas import tpu as pltpu
from jax.sharding import PartitionSpec as P

R = 128
F32 = jnp.float32
MERGES = 3


HIGHEST = lax.Precision.HIGHEST


SIDE = 4
MESH = pl.DeviceIdType.MESH


def place_of():
    clus = lax.axis_index("clus")
    return (clus // 8, clus // 2 % SIDE, clus % 2)


def clus_at(z, y, core):
    return {"clus": (z % SIDE * SIDE + y % SIDE) * 2 + core}


def remote(src, dst, send, recv, device):
    return pltpu.make_async_remote_copy(
        src_ref=src, dst_ref=dst, send_sem=send, recv_sem=recv, device_id=device, device_id_type=MESH
    )


def meet(devices):
    barrier = pltpu.get_barrier_semaphore()
    for device in devices:
        pl.semaphore_signal(barrier, inc=1, device_id=device, device_id_type=MESH)
    pl.semaphore_wait(barrier, len(devices))


def sample_kernel(
    near, op_hbm, omega_hbm, q_hbm, lead_out, gram_out,
    op, own, away, fromcore, zin, yin, zpart, ypart, zlast, ylast, gathered, total, vsend, vin,
    op_sem, ag_send, ag_recv, fw_send, fw_recv, core_send, core_recv,
    rs_send, rs_recv, last_send, last_recv, v_send, v_recv,
    omega, q_own, u_sum, grams, part_in, pair_own, pair_in,
    in_sem, part_send, part_recv, pair_send, pair_recv, spread_send, spread_recv,
):
    z, y, core = place_of()
    x = lax.axis_index("row")
    here = z * SIDE + y
    other = 1 - core
    half = (pl.ds(0, 128), pl.ds(128, 128))
    steps = (1, 2, 3)
    me = lax.axis_index("clus")

    def far(t):
        is_near = (near[t, 0] == me) | (near[t, 1] == me) | (near[t, 2] == me)
        return jnp.where(is_near, 0.0, 1.0)

    def load(t):
        return pltpu.make_async_copy(op_hbm.at[t], op.at[t], op_sem.at[t])

    def spot(a, b):
        return (z - a + SIDE) % SIDE * SIDE + (y - b + SIDE) % SIDE

    def gather_send(h, a, b, along):
        piece = gathered.at[core, spot(a, b), half[h]]
        if h == 0:
            return remote(piece, piece, ag_send.at[h, along, b], ag_recv.at[h, along, b], clus_at(z + along, y, core))
        return remote(piece, piece, ag_send.at[h, a, along], ag_recv.at[h, a, along], clus_at(z, y + along, core))

    def gather_first(h, along):
        piece = gathered.at[core, here, half[h]]
        if h == 0:
            return remote(piece, piece, ag_send.at[h, 0, along], ag_recv.at[h, 0, along], clus_at(z, y + along, core))
        return remote(piece, piece, ag_send.at[h, along, 0], ag_recv.at[h, along, 0], clus_at(z + along, y, core))

    def arrived(h, a, b):
        piece = gathered.at[core, spot(a, b), half[h]]
        return remote(piece, piece, ag_send.at[h, a, b], ag_recv.at[h, a, b], clus_at(z, y, other))

    def forward(which, h, a, b):
        piece = gathered.at[which, spot(a, b), half[h]]
        return remote(piece, piece, fw_send.at[h, a, b], fw_recv.at[h, a, b], clus_at(z, y, other))

    def to_core(i):
        return remote(away.at[i], fromcore.at[i], core_send.at[i], core_recv.at[i], clus_at(z, y, other))

    def scatter(h, a, b):
        zt, yt = (z + a) % SIDE, (y + b) % SIDE
        block = own.at[zt * SIDE + yt, half[h]]
        if h == 0:
            return remote(block, zin.at[a, yt], rs_send.at[h, a, b], rs_recv.at[h, a, b], clus_at(zt, y, core))
        return remote(block, yin.at[b, zt], rs_send.at[h, a, b], rs_recv.at[h, a, b], clus_at(z, yt, core))

    def scatter_last(h, along):
        if h == 0:
            yt = (y + along) % SIDE
            return remote(zpart.at[yt], ylast.at[along], last_send.at[h, along], last_recv.at[h, along], clus_at(z, yt, core))
        zt = (z + along) % SIDE
        return remote(ypart.at[zt], zlast.at[along], last_send.at[h, along], last_recv.at[h, along], clus_at(zt, y, core))

    def row_send(along):
        xt = (x + along) % SIDE
        return remote(vsend.at[xt], vin.at[along], v_send.at[along], v_recv.at[along], {"row": xt})

    def part_at(along, which):
        xt = (x + along) % SIDE
        device = {"row": xt, "clus": (here * 2 + which)}
        return remote(
            grams.at[which, pl.ds(pl.multiple_of(xt * 32, 32), 32)], part_in.at[along, core],
            part_send.at[along, which], part_recv.at[along, core], device,
        )

    def part_from(along, which):
        return remote(
            part_in.at[along, which], part_in.at[along, which],
            part_send.at[along, which], part_recv.at[along, which], {"row": (x - along + SIDE) % SIDE},
        )

    def pair_at(along):
        return remote(
            pair_own, pair_in.at[along], pair_send.at[along], pair_recv.at[along], clus_at(z, y + along, core)
        )

    def spread(stage, along, which):
        xt = (x + along) % SIDE
        piece = gram_out.at[core, pl.ds((0, 2)[stage], (2, 3)[stage]), pl.ds(pl.multiple_of(x * 32, 32), 32)]
        return remote(
            piece, piece, spread_send.at[stage, along, which], spread_recv.at[stage, along, core],
            {"row": xt, "clus": here * 2 + which},
        )

    def spread_from(stage, along, which):
        xs = (x - along + SIDE) % SIDE
        piece = gram_out.at[which, pl.ds((0, 2)[stage], (2, 3)[stage]), pl.ds(pl.multiple_of(xs * 32, 32), 32)]
        return remote(
            piece, piece, spread_send.at[stage, along, which], spread_recv.at[stage, along, which],
            {"row": xs},
        )

    def both_cores(act):
        for d in (0, 1, 3, 2):
            if d:
                act(d, core)
            act(d, other)

    omega_in = pltpu.make_async_copy(omega_hbm, omega, in_sem.at[0])
    q_in = pltpu.make_async_copy(q_hbm, q_own, in_sem.at[1])
    q_in.start()
    omega_in.start()

    def loads(i, _):
        load(2 * i + other).start()
        load(2 * i + core).start()
        return 0

    lax.fori_loop(0, 16, loads, 0)
    meet(
        [clus_at(z, y, other)]
        + [clus_at(z, y + d, core) for d in steps]
        + [clus_at(z + d, y, core) for d in steps]
        + [{"row": (x + d) % SIDE, "clus": here * 2 + which} for d in steps for which in (core, other)]
    )
    q_in.wait()
    gathered[core, here] = q_own[...].astype(F32).T.astype(jnp.bfloat16)
    for d in (1, 3, 2):
        for h in range(2):
            gather_first(h, d).start()
    for d in (1, 3, 2):
        for h in range(2):
            gather_send(h, 0, 0, d).start()
    for h in range(2):
        forward(core, h, 0, 0).start()

    omega_in.wait()

    def column(i, _):
        for which, keep in ((other, away), (core, own)):
            t = 2 * i + which
            load(t).wait()
            product = jnp.dot(op[t], omega[...], preferred_element_type=F32) * far(t)
            keep[i] = product.astype(jnp.bfloat16)
            if keep is away:
                to_core(i).start()
        return 0

    lax.fori_loop(0, 8, column, 0)
    for d in (1, 3, 2):
        for h, a, b in ((0, 0, d), (1, d, 0)):
            arrived(h, a, b).wait_recv()
            for along in (1, 3, 2):
                gather_send(h, a, b, along).start()
            forward(core, h, a, b).start()
    lax.fori_loop(8, 16, column, 0)

    def pair_sum(i, _):
        a, b = i // SIDE, i % SIDE
        at = (z + a) % SIDE * SIDE + (y + b) % SIDE
        to_core(at).wait_recv()
        own[at] = (own[at].astype(F32) + fromcore[at].astype(F32)).astype(jnp.bfloat16)

        @pl.when(a != 0)
        def _():
            scatter(0, a, b).start()

        @pl.when(b != 0)
        def _():
            scatter(1, a, b).start()

        return 0

    lax.fori_loop(0, 16, pair_sum, 0)
    total[...] = jnp.zeros_like(total)

    def row_step(which, at):
        t = 2 * at + which
        piece = (gathered[which, at].astype(F32) * far(t)).astype(jnp.bfloat16)
        total[...] += jnp.dot(piece, op[t], preferred_element_type=F32)

    def row_own(i, _):
        a, b = i // SIDE, i % SIDE

        @pl.when(a != 0)
        def _():
            arrived(0, a, b).wait_recv()
            forward(core, 0, a, b).start()

        @pl.when(b != 0)
        def _():
            arrived(1, a, b).wait_recv()
            forward(core, 1, a, b).start()

        row_step(core, spot(a, b))
        return 0

    lax.fori_loop(0, 16, row_own, 0)

    def row_other(i, _):
        a, b = i // SIDE, i % SIDE
        for h in range(2):
            forward(other, h, a, b).wait_recv()
        row_step(other, spot(a, b))
        return 0

    lax.fori_loop(0, 16, row_other, 0)
    for quarter in range(SIDE):
        vsend[quarter] = total[:, quarter * 256:(quarter + 1) * 256].astype(jnp.bfloat16)
    for d in (1, 3, 2):
        row_send(d).start()

    def first_sum(i, _):
        yt = (y + i) % SIDE
        for d in steps:
            scatter(0, d, i).wait_recv()
        part = own[z * SIDE + yt, half[0]].astype(F32)
        for d in steps:
            part = part + zin[d, yt].astype(F32)
        zpart[yt] = part.astype(jnp.bfloat16)

        @pl.when(i == 0)
        def _():
            u_sum[half[0], :] = part

        zt = (z + i) % SIDE
        for d in steps:
            scatter(1, i, d).wait_recv()
        part = own[zt * SIDE + y, half[1]].astype(F32)
        for d in steps:
            part = part + yin[d, zt].astype(F32)
        ypart[zt] = part.astype(jnp.bfloat16)

        @pl.when(i == 0)
        def _():
            u_sum[half[1], :] = part

        @pl.when(i != 0)
        def _():
            scatter_last(0, i).start()
            scatter_last(1, i).start()

        return 0

    lax.fori_loop(0, SIDE, first_sum, 0)
    for d in steps:
        row_send(d).wait_recv()
    share = total[:, pl.ds(pl.multiple_of(x * 256, 256), 256)]
    for d in steps:
        share = share + vin[d].astype(F32)
    lead_out[1] = share[:R, :].T
    grams[1] = lax.dot_general(
        share[:R, :], share, (((1,), (1,)), ((), ())), precision=HIGHEST, preferred_element_type=F32
    )
    for h in range(2):
        late = (ylast, zlast)[h]
        for d in steps:
            scatter_last(h, d).wait_recv()
        part = u_sum[half[h], :]
        for d in steps:
            part = part + late[d].astype(F32)
        u_sum[half[h], :] = part
    lead_out[0] = u_sum[:, :R]
    grams[0] = lax.dot_general(
        u_sum[:, :R], u_sum[...], (((0,), (0,)), ((), ())), precision=HIGHEST, preferred_element_type=F32
    )
    both_cores(lambda d, which: part_at(d, which).start())
    part_in[0, core] = grams[core, pl.ds(pl.multiple_of(x * 32, 32), 32)]
    both_cores(lambda d, which: part_from(d, which).wait_recv())
    my_rows = pl.ds(pl.multiple_of(x * 32, 32), 32)
    leaf = [part_in[0, s] + part_in[1, s] + part_in[2, s] + part_in[3, s] for s in range(2)]
    pair = leaf[0] + leaf[1]
    pair_own[...] = pair
    for d in (1, 3, 2):
        pair_at(d).start()
    for s in range(2):
        gram_out[core, s, my_rows] = leaf[s][:, :R]
    both_cores(lambda d, which: spread(0, d, which).start())
    for d in steps:
        pair_at(d).wait_recv()
    odd = y % 2
    near_pair = pair_in[3 - 2 * odd]
    far_pair = pair_in[2] + pair_in[1 + 2 * odd]
    gram_out[core, 2, my_rows] = near_pair[:, :R]
    gram_out[core, 3, my_rows] = far_pair[:, :R]
    gram_out[core, 4, my_rows] = ((pair + near_pair) + far_pair)[:, R:]
    both_cores(lambda d, which: spread(1, d, which).start())
    for stage in range(2):
        both_cores(lambda d, which: spread_from(stage, d, which).wait_recv())

    both_cores(lambda d, which: part_at(d, which).wait_send())
    for stage in range(2):
        both_cores(lambda d, which: spread(stage, d, which).wait_send())
    for d in steps:
        pair_at(d).wait_send()
    for d in steps:
        row_send(d).wait_send()
        for h in range(2):
            gather_first(h, d).wait_send()
            scatter_last(h, d).wait_send()

    def drain(i, _):
        a, b = i // SIDE, i % SIDE
        to_core(i).wait_send()
        for h in range(2):
            forward(core, h, a, b).wait_send()

        @pl.when(a != 0)
        def _():
            arrived(0, a, b).wait_send()
            scatter(0, a, b).wait_send()

        @pl.when(b != 0)
        def _():
            arrived(1, a, b).wait_send()
            scatter(1, a, b).wait_send()

        return 0

    lax.fori_loop(0, 16, drain, 0)


def grams_of(near_list, operator, omega, omega_rows):
    vmem = pl.BlockSpec(memory_space=pltpu.VMEM)
    anywhere = pl.BlockSpec(memory_space=pl.ANY)
    bf16 = jnp.bfloat16
    sem = pltpu.SemaphoreType.DMA
    block = (256, 256)
    part = (128, 256)
    return pl.pallas_call(
        sample_kernel,
        out_shape=[jax.ShapeDtypeStruct((2, 256, R), F32), jax.ShapeDtypeStruct((2, 5, R, R), F32)],
        in_specs=[pl.BlockSpec(memory_space=pltpu.SMEM), anywhere, anywhere, anywhere],
        out_specs=[vmem, vmem],
        scratch_shapes=[
            pltpu.VMEM(operator.shape, bf16),
            pltpu.VMEM((16, *block), bf16),
            pltpu.VMEM((16, *block), bf16),
            pltpu.VMEM((16, *block), bf16),
            pltpu.VMEM((SIDE, SIDE, *part), bf16),
            pltpu.VMEM((SIDE, SIDE, *part), bf16),
            pltpu.VMEM((SIDE, *part), bf16),
            pltpu.VMEM((SIDE, *part), bf16),
            pltpu.VMEM((SIDE, *part), bf16),
            pltpu.VMEM((SIDE, *part), bf16),
            pltpu.VMEM((2, 16, *block), bf16),
            pltpu.VMEM((256, 1024), F32),
            pltpu.VMEM((SIDE, *block), bf16),
            pltpu.VMEM((SIDE, *block), bf16),
            sem((32,)),
            sem((2, SIDE, SIDE)),
            sem((2, SIDE, SIDE)),
            sem((2, SIDE, SIDE)),
            sem((2, SIDE, SIDE)),
            sem((16,)),
            sem((16,)),
            sem((2, SIDE, SIDE)),
            sem((2, SIDE, SIDE)),
            sem((2, SIDE)),
            sem((2, SIDE)),
            sem((SIDE,)),
            sem((SIDE,)),
            pltpu.VMEM(omega.shape, bf16),
            pltpu.VMEM(block, bf16),
            pltpu.VMEM(block, F32),
            pltpu.VMEM((2, R, 256), F32),
            pltpu.VMEM((SIDE, 2, 32, 256), F32),
            pltpu.VMEM((32, 256), F32),
            pltpu.VMEM((SIDE, 32, 256), F32),
            sem((2,)),
            sem((SIDE, 2)),
            sem((SIDE, 2)),
            sem((SIDE,)),
            sem((SIDE,)),
            sem((2, SIDE, 2)),
            sem((2, SIDE, 2)),
        ],
        compiler_params=pltpu.CompilerParams(
            collective_id=0, has_side_effects=True, vmem_limit_bytes=48 << 20
        ),
        cost_estimate=pl.CostEstimate(flops=1 << 33, bytes_accessed=1 << 24, transcendentals=0),
    )(near_list, operator, omega, omega_rows)


def split3(x):
    hi = x.astype(jnp.bfloat16).astype(F32)
    rest = x - hi
    mid = rest.astype(jnp.bfloat16).astype(F32)
    low = rest - mid
    return hi, mid, low

def panel(state, m, first):
    rows = state[m, first:first + 8, :]
    place = lax.broadcasted_iota(jnp.int32, (8, R), 0)
    place2 = lax.broadcasted_iota(jnp.int32, (8, 2 * R), 0)
    cols = [jnp.broadcast_to(rows[:, first + c:first + c + 1], (8, R)) for c in range(8)]
    for c in range(8):
        scale = lax.rsqrt(jnp.broadcast_to(cols[c][c:c + 1, :], (8, R)))
        mult = jnp.where(place > c, cols[c] * scale, 0.0)
        for k in range(c + 1, 8):
            cols[k] = cols[k] - mult * (jnp.broadcast_to(cols[k][c:c + 1, :], (8, R)) * scale)
        scale2 = jnp.concatenate([scale, scale], axis=1)
        mult2 = jnp.concatenate([mult, mult], axis=1)
        pivot = jnp.broadcast_to(rows[c:c + 1, :], (8, 2 * R)) * scale2
        rows = jnp.where(place2 == c, pivot, rows - mult2 * pivot)
    state[m, first:first + 8, :] = rows
    last = first + 8
    if last < R:
        hi, mid, low = split3(rows)
        left = jnp.concatenate([hi, hi, mid, mid, hi, low], axis=0).astype(jnp.bfloat16)
        right = jnp.concatenate([hi, mid, hi, mid, low, hi], axis=0).astype(jnp.bfloat16)
        state[m, last:, :] -= lax.dot_general(left[:, last:R] if last % R == 0 else left[:, :R], right, (((0,), (0,)), ((), ())), preferred_element_type=F32)[last:, :]

def chol_all(state, count):
    for first in range(0, R, 8):
        for m in range(count):
            panel(state, m, first)

def factor_kernel(gram_ref, lead_ref, ub_ref, vb_ref, ut_ref, vt_ref, utop_ref, vtop_ref, state):
    _, y, core = place_of()
    eye_rows = lax.broadcasted_iota(jnp.int32, (R, R), 0)
    eye_cols = lax.broadcasted_iota(jnp.int32, (R, R), 1)
    eye = (eye_rows == eye_cols).astype(F32)
    low, high = y % 2, y // 2
    for s in range(2):
        at = 7 * s
        first, second, near_pair, far_pair = (gram_ref[s, i] for i in range(4))
        pair = first + second
        quad = pair + near_pair
        state[at, :, :R] = first
        state[at + 1, :, :R] = second
        state[at + 2 + low, :, :R] = pair
        state[at + 3 - low, :, :R] = near_pair
        state[at + 4 + high, :, :R] = quad
        state[at + 5 - high, :, :R] = far_pair
        state[at + 6, :, :R] = quad + far_pair
        for i in range(7):
            state[at + i, :, R:] = eye
    chol_all(state, 14)
    for m in range(14):
        state[m, :, :R] = jnp.where(eye_cols >= eye_rows, state[m, :, :R], 0.0)
    outer = (((1,), (1,)), ((), ()))
    for s in range(2):
        basis_ref, trans_ref, top_ref = ((ub_ref, ut_ref, utop_ref), (vb_ref, vt_ref, vtop_ref))[s]
        at = 7 * s
        basis_ref[...] = lax.dot_general(
            lead_ref[s], state[at + core, :, R:] * math.sqrt(1024), outer,
            precision=HIGHEST, preferred_element_type=F32,
        )
        for k in range(MERGES):
            parent = at + (2 + low, 4 + high, 6)[k]
            inverse = state[parent, :, R:] * math.sqrt(2 * R)
            for h in range(2):
                trans_ref[0, k, h * R:(h + 1) * R, :] = lax.dot_general(
                    state[at + 2 * k + h, :, :R], inverse, outer, precision=HIGHEST, preferred_element_type=F32
                )
        top_ref[0, :, :R] = state[at + 6, :, :R] * (1.0 / math.sqrt(1024))
        top_ref[0, :, R:] = jnp.dot(
            state[at + 6, :, R:], gram_ref[s, 4], precision=HIGHEST, preferred_element_type=F32
        ) * (1.0 / math.sqrt(1024))


def factor_all(grams, leading):
    vmem = pl.BlockSpec(memory_space=pltpu.VMEM)
    shapes = [(256, R)] * 2 + [(1, MERGES, 2 * R, R)] * 2 + [(1, R, 2 * R)] * 2
    return pl.pallas_call(
        factor_kernel,
        out_shape=[jax.ShapeDtypeStruct(shape, F32) for shape in shapes],
        in_specs=[vmem, vmem],
        out_specs=[vmem] * 6,
        scratch_shapes=[pltpu.VMEM((14, R, 2 * R), F32)],
        compiler_params=pltpu.CompilerParams(vmem_limit_bytes=40 << 20),
    )(grams, leading)


def body(operator, omega, omega_rows, near_list):
    leading, grams = grams_of(near_list, operator, omega, omega_rows)
    return tuple(factor_all(grams, leading))


def solution(mesh):
    in_specs = (P(None, "row", "clus"), P("clus", None), P(("clus", "row"), None), P())
    out_specs = (
        P(("clus", "row"), None),
        P(("clus", "row"), None),
        P("clus", None, None, None),
        P("clus", None, None, None),
        P("clus", None, None),
        P("clus", None, None),
    )
    return jax.shard_map(body, mesh=mesh, in_specs=in_specs, out_specs=out_specs, check_vma=False)
```

```python
import math

import jax
import jax.numpy as jnp
from jax import lax
from jax.experimental import pallas as pl
from jax.experimental.pallas import tpu as pltpu
from jax.sharding import PartitionSpec as P

R = 128
F32 = jnp.float32
MERGES = 3


HIGHEST = lax.Precision.HIGHEST


SIDE = 4
MESH = pl.DeviceIdType.MESH
BF16 = jnp.bfloat16
BACK = (3, 1)
EARLY = 2


def place_of():
    clus = lax.axis_index("clus")
    return (clus // 8, clus // 2 % SIDE, clus % 2)


def clus_at(z, y, core):
    return {"clus": (z % SIDE * SIDE + y % SIDE) * 2 + core}


def remote(src, dst, send, recv, device):
    return pltpu.make_async_remote_copy(
        src_ref=src, dst_ref=dst, send_sem=send, recv_sem=recv, device_id=device, device_id_type=MESH
    )


def greet(devices):
    for device in devices:
        pl.semaphore_signal(pltpu.get_barrier_semaphore(), inc=1, device_id=device, device_id_type=MESH)


def sample_kernel(
    near_hbm, op_hbm, omega_hbm, q_hbm, lead_out, gram_out,
    near, weights, op, omega, q_own, own, away, fromcore, far_in, near_in, parts, last_in, gathered, wide, total,
    vsend, vin, u_sum, grams, part_in, pair_own, pair_in,
    in_sem, op_sem, ag1_s, ag1_r, ag2_s, ag2_r, ag2x_s, ag2x_r, fw_s, fw_r, core_s, core_r,
    far_s, far_r, near_s, near_r, last_s, last_r, v_s, v_r,
    part_s, part_r, pair_s, pair_r, spread_s, spread_r, share_s, share_r,
):
    z, y, core = place_of()
    x = lax.axis_index("row")
    me = lax.axis_index("clus")
    here = z * SIDE + y
    other = 1 - core
    steps = (1, 2, 3)
    half = (pl.ds(0, 128), pl.ds(128, 128))
    pieces = tuple(tuple(pl.ds(128 * h + 64 * s, 64) for s in range(2)) for h in range(2))
    ahead = (1, 3)

    def far(t):
        return weights[pl.ds(t, 1), :]

    def spot(h, d1, d2):
        dz, dy = (d2, d1) if h == 0 else (d1, d2)
        return (z + dz) % SIDE * SIDE + (y + dy) % SIDE

    def along_y(d):
        return clus_at(z, y + d, core)

    def along_z(d):
        return clus_at(z + d, y, core)

    first = (along_y, along_z)
    second = (along_z, along_y)

    def same(ref, send, recv, device):
        return remote(ref, ref, send, recv, device)

    def ag1(h, d, d1=0):
        return same(gathered.at[core, spot(h, d1, 0), half[h]], ag1_s.at[h, d], ag1_r.at[h, d], first[h](d))

    def ag2(h, e, s, d2=0):
        return same(gathered.at[core, spot(h, e, d2), half[h]], ag2_s.at[h, e, s], ag2_r.at[h, e, s], second[h](ahead[s]))

    def ag2x(h, e, s, d2):
        return same(gathered.at[core, spot(h, e, d2), pieces[h][s]], ag2x_s.at[h, e, s], ag2x_r.at[h, e, s], second[h](ahead[s]))

    def forward(which, h, d1, d2):
        return same(gathered.at[which, spot(h, d1, d2), half[h]], fw_s.at[h, d1, d2], fw_r.at[h, d1, d2], clus_at(z, y, other))

    def to_core(i):
        return remote(away.at[i], fromcore.at[i], core_s.at[i], core_r.at[i], clus_at(z, y, other))

    def block(h, d, i):
        return (z + d) % SIDE * SIDE + i if h == 0 else i * SIDE + (y + d) % SIDE

    def far_send(h, s, i):
        return remote(own.at[block(h, 2, i), pieces[h][s]], far_in.at[h, s, i], far_s.at[h, s, i], far_r.at[h, s, i], second[h](ahead[s]))

    def near_send(h, s, i):
        return remote(own.at[block(h, ahead[s], i), half[h]], near_in.at[h, s, i], near_s.at[h, s, i], near_r.at[h, s, i], second[h](ahead[s]))

    def last_send(h, d):
        i = ((y if h == 0 else z) + d) % SIDE
        return remote(parts.at[h, i], last_in.at[h, d], last_s.at[h, d], last_r.at[h, d], first[h](d))

    def row_at(d, which=None):
        xt = (x + d) % SIDE
        return {"row": xt} if which is None else {"row": xt, "clus": here * 2 + which}

    def row_send(d):
        return remote(vsend.at[d], vin.at[d], v_s.at[d], v_r.at[d], row_at(d))

    def rows32(d):
        return pl.ds(pl.multiple_of((x + d) % SIDE * 32, 32), 32)

    def part_at(d, which):
        return remote(
            grams.at[which, rows32(d)], part_in.at[d, core], part_s.at[d, which], part_r.at[d, core], row_at(d, which)
        )

    def part_from(d, which):
        return same(part_in.at[d, which], part_s.at[d, which], part_r.at[d, which], row_at(SIDE - d))

    def pair_at(d):
        return remote(pair_own, pair_in.at[d], pair_s.at[d], pair_r.at[d], along_y(d))

    slots = (pl.ds(0, 2), pl.ds(2, 3))

    def spread(k, d, d_from=0):
        return same(gram_out.at[core, slots[k], rows32(d_from)], spread_s.at[k, d], spread_r.at[k, d], row_at(d))

    def share(which, k, d):
        return same(gram_out.at[which, slots[k], rows32(d)], share_s.at[k, d], share_r.at[k, d], clus_at(z, y, other))

    def both_cores(act):
        for d in (0, 1, 3, 2):
            if d:
                act(d, core)
            act(d, other)

    def group_at(i):
        return (z + 2 + i // 2) % SIDE * 2 + (y // 2 + 1 + i) % 2

    def load(g):
        return pltpu.make_async_copy(op_hbm.at[pl.ds(4 * g, 4)], op.at[pl.ds(4 * g, 4)], op_sem.at[g])

    partners = (
        [clus_at(z, y, other)]
        + [along_y(d) for d in steps]
        + [along_z(d) for d in steps]
        + [row_at(d, which) for d in steps for which in (core, other)]
    )
    greet(partners)
    omega_in = pltpu.make_async_copy(omega_hbm, omega, in_sem.at[0])
    q_in = pltpu.make_async_copy(q_hbm, q_own, in_sem.at[1])
    near_in_copy = pltpu.make_async_copy(near_hbm, near, in_sem.at[2])
    near_in_copy.start()
    omega_in.start()

    def start_load(i, _):
        load(group_at(i)).start()
        return 0

    lax.fori_loop(0, 8, start_load, 0)
    q_in.start()
    near_in_copy.wait()
    is_near = jnp.max((near[...] == me).astype(F32), axis=0, keepdims=True)
    count = near.shape[1]
    on_row = lax.broadcasted_iota(jnp.int32, (count, count), 0) == lax.broadcasted_iota(jnp.int32, (count, count), 1)
    near_rows = jnp.sum(jnp.where(on_row, jnp.broadcast_to(is_near, (count, count)), 0.0), axis=1, keepdims=True)
    weights[...] = jnp.broadcast_to(1.0 - near_rows, weights.shape)
    omega_in.wait()

    def begin():
        q_in.wait()
        gathered[core, here] = q_own[...].astype(F32).T.astype(BF16)
        pl.semaphore_wait(pltpu.get_barrier_semaphore(), len(partners))
        for d in (2, 1, 3):
            for h in range(2):
                ag1(h, d).start()
        for h in range(2):
            for s in range(2):
                ag2(h, 0, s).start()
        for h in range(2):
            forward(core, h, 0, 0).start()

    def first_in(d):
        for h in range(2):
            ag1(h, d, SIDE - d).wait_recv()
            for s in range(2):
                ag2(h, SIDE - d, s).start()
            forward(core, h, SIDE - d, 0).start()

    def second_in(e):
        for h in range(2):
            for s in range(2):
                ag2(h, e, s, BACK[s]).wait_recv()
                ag2x(h, e, s, BACK[s]).start()
                forward(core, h, e, BACK[s]).start()

    def second_opposite_in(e):
        for h in range(2):
            for s in range(2):
                ag2x(h, e, s, 2).wait_recv()
            forward(core, h, e, 2).start()

    def column(i):
        g = group_at(i)
        load(g).wait()
        product = jnp.dot(
            op[pl.ds(4 * g, 4)].reshape(1024, 1024), omega[...], preferred_element_type=F32
        )
        for j in range(2):
            for which in range(2):
                n = 2 * j + which
                term = (product[256 * n:256 * n + 256] * far(4 * g + n)).astype(BF16)

                @pl.when(core == which)
                def _():
                    own[2 * g + j] = term

                @pl.when(core != which)
                def _():
                    away[2 * g + j] = term


    def column_early(i, _):
        column(i)
        return 0

    def column_late(i, _):
        column(i)
        for j in range(2):
            to_core(2 * group_at(i) + j).start()
        return 0

    lax.fori_loop(0, EARLY, column_early, 0)
    begin()

    def send_early(i, _):
        for j in range(2):
            to_core(2 * group_at(i) + j).start()
        return 0

    lax.fori_loop(0, EARLY, send_early, 0)
    lax.fori_loop(EARLY, 8, column_late, 0)

    def pair_sum(i, _):
        g = group_at(i)
        for j in range(2):
            at = 2 * g + j
            to_core(at).wait_recv()
            own[at] = (own[at].astype(F32) + fromcore[at].astype(F32)).astype(BF16)
            zt, yt = at // SIDE, at % SIDE

            @pl.when(zt == (z + 2) % SIDE)
            def _():
                for s in range(2):
                    far_send(0, s, yt).start()

            @pl.when(yt == (y + 2) % SIDE)
            def _():
                for s in range(2):
                    far_send(1, s, zt).start()

        return 0

    lax.fori_loop(0, 8, pair_sum, 0)
    for d in (1, 3, 2):
        first_in(d)
    second_in(0)

    def add_far(i, _):
        for h in range(2):
            for s in range(2):
                far_send(h, s, i).wait_recv()
                at = block(h, ahead[s], i)
                own[at, pieces[h][s]] = (own[at, pieces[h][s]].astype(F32) + far_in[h, s, i].astype(F32)).astype(BF16)
                near_send(h, s, i).start()
        return 0

    lax.fori_loop(0, SIDE, add_far, 0)
    for e in (3, 1, 2):
        second_in(e)
    total[...] = jnp.zeros_like(total)

    def scaled(a, b):
        forward(other, 0, b, a).wait_recv()
        forward(other, 1, a, b).wait_recv()
        at = spot(0, b, a)
        return jnp.concatenate(
            [(gathered[which, at].astype(F32) * far(2 * at + which)).astype(BF16) for which in range(2)], axis=1
        )

    def row_step(i, _):
        a, b = i // 3 + i // 3 // 2, i % 3 + i % 3 // 2
        both = op[pl.ds(2 * spot(0, b, a), 2)].reshape(512, 1024)
        total[...] += jnp.dot(scaled(a, b), both, preferred_element_type=F32)
        return 0

    lax.fori_loop(0, 9, row_step, 0)
    for e in (0, 3, 1, 2):
        second_opposite_in(e)

    def late_place(i):
        j = i % 4
        return (2 * (1 - i // 4) + i // 4 * (j + j // 2), (1 - i // 4) * i + i // 4 * 2)

    def late_piece(i, _):
        wide[i] = scaled(*late_place(i))
        return 0

    lax.fori_loop(0, 7, late_piece, 0)

    def quarter(d):
        columns = pl.ds(pl.multiple_of((x + d) % SIDE * 256, 256), 256)

        running = total[:, columns]
        for i in range(7):
            a, b = late_place(i)
            both = op[pl.ds(2 * spot(0, b, a), 2), :, columns].reshape(512, 256)
            running = running + jnp.dot(wide[i], both, preferred_element_type=F32)
        return running

    def send_quarter(i, _):
        d = (2 + 3 * i + i // 2 * 3) % SIDE
        vsend[d] = quarter(d).astype(BF16)
        row_send(d).start()
        return 0

    def first_sum(i, _):
        for h in range(2):
            for s in range(2):
                near_send(h, s, i).wait_recv()
            part = own[block(h, 0, i), half[h]].astype(F32)
            for s in range(2):
                part = part + near_in[h, s, i].astype(F32)
            parts[h, i] = part.astype(BF16)

            @pl.when(i == (y, z)[h])
            def _():
                u_sum[half[h], :] = part

        return 0

    lax.fori_loop(0, SIDE, first_sum, 0)
    for d in (2, 1, 3):
        for h in range(2):
            last_send(h, d).start()
    lax.fori_loop(0, 3, send_quarter, 0)
    mine = quarter(0)
    for h in range(2):
        for d in steps:
            last_send(h, d).wait_recv()
        part = u_sum[half[h], :]
        for d in steps:
            part = part + last_in[h, d].astype(F32)
        u_sum[half[h], :] = part
    lead_out[0] = u_sum[:, :R]
    grams[0] = lax.dot_general(
        u_sum[:, :R], u_sum[...], (((0,), (0,)), ((), ())), precision=HIGHEST, preferred_element_type=F32
    )
    for d in (2, 1, 3):
        part_at(d, 0).start()
    for d in (2, 1, 3):
        row_send(d).wait_recv()
        mine = mine + vin[d].astype(F32)
    lead_out[1] = mine[:R, :].T
    grams[1] = lax.dot_general(
        mine[:R, :], mine, (((1,), (1,)), ((), ())), precision=HIGHEST, preferred_element_type=F32
    )
    for d in (2, 1, 3):
        part_at(d, 1).start()
    part_at(0, other).start()
    part_in[0, core] = grams[core, rows32(0)]
    both_cores(lambda d, which: part_from(d, which).wait_recv())
    leaf = [part_in[0, s] + part_in[1, s] + part_in[2, s] + part_in[3, s] for s in range(2)]
    pair = leaf[0] + leaf[1]
    pair_own[...] = pair
    for d in (2, 1, 3):
        pair_at(d).start()
    for s in range(2):
        gram_out[core, s, rows32(0)] = leaf[s][:, :R]

    def spread_out(k):
        for d in (2, 1, 3):
            spread(k, d).start()
        share(core, k, 0).start()

    def spread_in(k):
        for d in (1, 3, 2):
            spread(k, d, SIDE - d).wait_recv()
            share(core, k, SIDE - d).start()

    spread_out(0)
    for d in steps:
        pair_at(d).wait_recv()
    odd = y % 2
    near_pair = pair_in[3 - 2 * odd]
    far_pair = pair_in[2] + pair_in[1 + 2 * odd]
    gram_out[core, 2, rows32(0)] = near_pair[:, :R]
    gram_out[core, 3, rows32(0)] = far_pair[:, :R]
    gram_out[core, 4, rows32(0)] = ((pair + near_pair) + far_pair)[:, R:]
    spread_out(1)
    spread_in(0)
    spread_in(1)
    for k in range(2):
        for d in range(SIDE):
            share(other, k, d).wait_recv()

    for h in range(2):
        for s in range(2):
            for e in range(SIDE):
                ag2(h, e, s).wait_send()
                ag2x(h, e, s, BACK[s]).wait_send()

    def drain(i, _):
        for h in range(2):
            for s in range(2):
                far_send(h, s, i).wait_send()
                near_send(h, s, i).wait_send()
            for d in range(SIDE):
                forward(core, h, i, d).wait_send()
        for d in range(SIDE):
            to_core(SIDE * i + d).wait_send()
        return 0

    lax.fori_loop(0, SIDE, drain, 0)
    for d in steps:
        row_send(d).wait_send()
        for h in range(2):
            ag1(h, d).wait_send()
            last_send(h, d).wait_send()
        pair_at(d).wait_send()
    both_cores(lambda d, which: part_at(d, which).wait_send())
    for k in range(2):
        for d in steps:
            spread(k, d).wait_send()
        for d in range(SIDE):
            share(core, k, d).wait_send()


def grams_of(near_list, operator, omega, omega_rows):
    vmem = pl.BlockSpec(memory_space=pltpu.VMEM)
    sem = pltpu.SemaphoreType.DMA
    block = (256, 256)
    part = (128, 256)

    def buffer(*shape, dtype=BF16):
        return pltpu.VMEM(shape, dtype)

    def sems(*shape):
        return [sem(shape), sem(shape)]

    return pl.pallas_call(
        sample_kernel,
        out_shape=[jax.ShapeDtypeStruct((2, 256, R), F32), jax.ShapeDtypeStruct((2, 5, R, R), F32)],
        in_specs=[pl.BlockSpec(memory_space=pltpu.HBM)] * 4,
        out_specs=[vmem, vmem],
        scratch_shapes=[
            buffer(near_list.shape[1], near_list.shape[0], dtype=jnp.int32),
            buffer(operator.shape[0], 256, dtype=F32),
            buffer(*operator.shape),
            buffer(*omega.shape),
            buffer(*block),
            buffer(16, *block),
            buffer(16, *block),
            buffer(16, *block),
            buffer(2, 2, SIDE, 64, 256),
            buffer(2, 2, SIDE, *part),
            buffer(2, SIDE, *part),
            buffer(2, SIDE, *part),
            buffer(2, 16, *block),
            buffer(7, 256, 512),
            buffer(256, 1024, dtype=F32),
            buffer(SIDE, *block),
            buffer(SIDE, *block),
            buffer(*block, dtype=F32),
            buffer(2, R, 256, dtype=F32),
            buffer(SIDE, 2, 32, 256, dtype=F32),
            buffer(32, 256, dtype=F32),
            buffer(SIDE, 32, 256, dtype=F32),
            sem((3,)),
            sem((8,)),
            *sems(2, SIDE),
            *sems(2, SIDE, 2),
            *sems(2, SIDE, 2),
            *sems(2, SIDE, SIDE),
            *sems(16),
            *sems(2, 2, SIDE),
            *sems(2, 2, SIDE),
            *sems(2, SIDE),
            *sems(SIDE),
            *sems(SIDE, 2),
            *sems(SIDE),
            *sems(2, SIDE),
            *sems(2, SIDE),
        ],
        compiler_params=pltpu.CompilerParams(
            collective_id=0, has_side_effects=True, vmem_limit_bytes=52 << 20
        ),
        cost_estimate=pl.CostEstimate(flops=1 << 33, bytes_accessed=1 << 24, transcendentals=0),
    )(near_list.T, operator, omega, omega_rows)


def split3(x):
    hi = x.astype(jnp.bfloat16).astype(F32)
    rest = x - hi
    mid = rest.astype(jnp.bfloat16).astype(F32)
    low = rest - mid
    return hi, mid, low

def panel(state, m, first):
    rows = state[m, first:first + 8, :]
    place = lax.broadcasted_iota(jnp.int32, (8, R), 0)
    place2 = lax.broadcasted_iota(jnp.int32, (8, 2 * R), 0)
    cols = [jnp.broadcast_to(rows[:, first + c:first + c + 1], (8, R)) for c in range(8)]
    for c in range(8):
        scale = lax.rsqrt(jnp.broadcast_to(cols[c][c:c + 1, :], (8, R)))
        mult = jnp.where(place > c, cols[c] * scale, 0.0)
        for k in range(c + 1, 8):
            cols[k] = cols[k] - mult * (jnp.broadcast_to(cols[k][c:c + 1, :], (8, R)) * scale)
        scale2 = jnp.concatenate([scale, scale], axis=1)
        mult2 = jnp.concatenate([mult, mult], axis=1)
        pivot = jnp.broadcast_to(rows[c:c + 1, :], (8, 2 * R)) * scale2
        rows = jnp.where(place2 == c, pivot, rows - mult2 * pivot)
    state[m, first:first + 8, :] = rows
    last = first + 8
    if last < R:
        hi, mid, low = split3(rows)
        left = jnp.concatenate([hi, hi, mid, mid, hi, low], axis=0).astype(jnp.bfloat16)
        right = jnp.concatenate([hi, mid, hi, mid, low, hi], axis=0).astype(jnp.bfloat16)
        state[m, last:, :] -= lax.dot_general(left[:, last:R] if last % R == 0 else left[:, :R], right, (((0,), (0,)), ((), ())), preferred_element_type=F32)[last:, :]

def chol_all(state, count):
    for first in range(0, R, 8):
        for m in range(count):
            panel(state, m, first)

def factor_kernel(gram_ref, lead_ref, ub_ref, vb_ref, ut_ref, vt_ref, utop_ref, vtop_ref, state):
    _, y, core = place_of()
    eye_rows = lax.broadcasted_iota(jnp.int32, (R, R), 0)
    eye_cols = lax.broadcasted_iota(jnp.int32, (R, R), 1)
    eye = (eye_rows == eye_cols).astype(F32)
    low, high = y % 2, y // 2
    for s in range(2):
        at = 7 * s
        first, second, near_pair, far_pair = (gram_ref[s, i] for i in range(4))
        pair = first + second
        quad = pair + near_pair
        state[at, :, :R] = first
        state[at + 1, :, :R] = second
        state[at + 2 + low, :, :R] = pair
        state[at + 3 - low, :, :R] = near_pair
        state[at + 4 + high, :, :R] = quad
        state[at + 5 - high, :, :R] = far_pair
        state[at + 6, :, :R] = quad + far_pair
        for i in range(7):
            state[at + i, :, R:] = eye
    chol_all(state, 14)
    for m in range(14):
        state[m, :, :R] = jnp.where(eye_cols >= eye_rows, state[m, :, :R], 0.0)
    outer = (((1,), (1,)), ((), ()))
    for s in range(2):
        basis_ref, trans_ref, top_ref = ((ub_ref, ut_ref, utop_ref), (vb_ref, vt_ref, vtop_ref))[s]
        at = 7 * s
        basis_ref[...] = lax.dot_general(
            lead_ref[s], state[at + core, :, R:] * math.sqrt(1024), outer,
            precision=HIGHEST, preferred_element_type=F32,
        )
        for k in range(MERGES):
            parent = at + (2 + low, 4 + high, 6)[k]
            inverse = state[parent, :, R:] * math.sqrt(2 * R)
            for h in range(2):
                trans_ref[0, k, h * R:(h + 1) * R, :] = lax.dot_general(
                    state[at + 2 * k + h, :, :R], inverse, outer, precision=HIGHEST, preferred_element_type=F32
                )
        top_ref[0, :, :R] = state[at + 6, :, :R] * (1.0 / math.sqrt(1024))
        top_ref[0, :, R:] = jnp.dot(
            state[at + 6, :, R:], gram_ref[s, 4], precision=HIGHEST, preferred_element_type=F32
        ) * (1.0 / math.sqrt(1024))


def factor_all(grams, leading):
    vmem = pl.BlockSpec(memory_space=pltpu.VMEM)
    shapes = [(256, R)] * 2 + [(1, MERGES, 2 * R, R)] * 2 + [(1, R, 2 * R)] * 2
    return pl.pallas_call(
        factor_kernel,
        out_shape=[jax.ShapeDtypeStruct(shape, F32) for shape in shapes],
        in_specs=[vmem, vmem],
        out_specs=[vmem] * 6,
        scratch_shapes=[pltpu.VMEM((14, R, 2 * R), F32)],
        compiler_params=pltpu.CompilerParams(vmem_limit_bytes=40 << 20),
    )(grams, leading)


def body(operator, omega, omega_rows, near_list):
    leading, grams = grams_of(near_list, operator, omega, omega_rows)
    return tuple(factor_all(grams, leading))


def solution(mesh):
    in_specs = (P(None, "row", "clus"), P("clus", None), P(("clus", "row"), None), P())
    out_specs = (
        P(("clus", "row"), None),
        P(("clus", "row"), None),
        P("clus", None, None, None),
        P("clus", None, None, None),
        P("clus", None, None),
        P("clus", None, None),
    )
    return jax.shard_map(body, mesh=mesh, in_specs=in_specs, out_specs=out_specs, check_vma=False)
```

```python
import math

import jax
import jax.numpy as jnp
from jax import lax
from jax.experimental import pallas as pl
from jax.experimental.pallas import tpu as pltpu
from jax.sharding import PartitionSpec as P

R = 128
F32 = jnp.float32
MERGES = 3


HIGHEST = lax.Precision.HIGHEST


SIDE = 4
MESH = pl.DeviceIdType.MESH
BF16 = jnp.bfloat16
BACK = (3, 1)
EARLY = 2


def place_of():
    clus = lax.axis_index("clus")
    return (clus // 8, clus // 2 % SIDE, clus % 2)


def clus_at(z, y, core):
    return {"clus": (z % SIDE * SIDE + y % SIDE) * 2 + core}


def remote(src, dst, send, recv, device):
    return pltpu.make_async_remote_copy(
        src_ref=src, dst_ref=dst, send_sem=send, recv_sem=recv, device_id=device, device_id_type=MESH
    )


def greet(devices):
    for device in devices:
        pl.semaphore_signal(pltpu.get_barrier_semaphore(), inc=1, device_id=device, device_id_type=MESH)


def sample_kernel(
    near_hbm, op_hbm, omega_hbm, q_hbm, lead_out, packed_out,
    near, weights, op, omega, q_own, own, away, fromcore, far_in, near_in, parts, last_in, gathered, wide, total,
    vsend, vin, u_sum, grams, part_in, pair_own, pair_in, sums, state,
    in_sem, op_sem, ag1_s, ag1_r, ag2_s, ag2_r, ag2x_s, ag2x_r, fw_s, fw_r, core_s, core_r,
    far_s, far_r, near_s, near_r, last_s, last_r, v_s, v_r,
    part_s, part_r, pair_s, pair_r, spread_s, spread_r, out_s, out_r,
):
    z, y, core = place_of()
    x = lax.axis_index("row")
    me = lax.axis_index("clus")
    here = z * SIDE + y
    other = 1 - core
    steps = (1, 2, 3)
    half = (pl.ds(0, 128), pl.ds(128, 128))
    pieces = tuple(tuple(pl.ds(128 * h + 64 * s, 64) for s in range(2)) for h in range(2))
    ahead = (1, 3)

    def far(t):
        return weights[pl.ds(t, 1), :]

    def spot(h, d1, d2):
        dz, dy = (d2, d1) if h == 0 else (d1, d2)
        return (z + dz) % SIDE * SIDE + (y + dy) % SIDE

    def along_y(d):
        return clus_at(z, y + d, core)

    def along_z(d):
        return clus_at(z + d, y, core)

    first = (along_y, along_z)
    second = (along_z, along_y)

    def same(ref, send, recv, device):
        return remote(ref, ref, send, recv, device)

    def ag1(h, d, d1=0):
        return same(gathered.at[core, spot(h, d1, 0), half[h]], ag1_s, ag1_r.at[h, d], first[h](d))

    def ag2(h, e, s, d2=0):
        return same(gathered.at[core, spot(h, e, d2), half[h]], ag2_s, ag2_r.at[h, e, s], second[h](ahead[s]))

    def ag2x(h, e, s, d2):
        return same(gathered.at[core, spot(h, e, d2), pieces[h][s]], ag2x_s, ag2x_r.at[h, e, s], second[h](ahead[s]))

    def forward(which, h, d1, d2):
        a, b = (d2, d1) if h == 0 else (d1, d2)
        return same(gathered.at[which, spot(h, d1, d2), half[h]], fw_s, fw_r.at[a, b], clus_at(z, y, other))

    def to_core(g):
        two = pl.ds(2 * g, 2)
        return remote(away.at[two], fromcore.at[two], core_s, core_r.at[g], clus_at(z, y, other))

    def wait_bytes(ref, sem):
        pltpu.make_async_copy(ref, ref, sem).wait()

    def block(h, d, i):
        return (z + d) % SIDE * SIDE + i if h == 0 else i * SIDE + (y + d) % SIDE

    def far_send(h, s, i):
        return remote(own.at[block(h, 2, i), pieces[h][s]], far_in.at[h, s, i], far_s, far_r, second[h](ahead[s]))

    def near_send(h, s, i):
        return remote(own.at[block(h, ahead[s], i), half[h]], near_in.at[h, s, i], near_s, near_r, second[h](ahead[s]))

    def last_send(h, d):
        i = ((y if h == 0 else z) + d) % SIDE
        return remote(parts.at[h, i], last_in.at[h, d], last_s, last_r.at[h], first[h](d))

    def row_at(d, which=None):
        xt = (x + d) % SIDE
        return {"row": xt} if which is None else {"row": xt, "clus": here * 2 + which}

    def row_send(d):
        return remote(vsend.at[d], vin.at[d], v_s, v_r, row_at(d))

    def rows32(d):
        return pl.ds(pl.multiple_of((x + d) % SIDE * 32, 32), 32)

    def part_at(d, which):
        return remote(grams.at[which, rows32(d)], part_in.at[2 * d + core], part_s, part_r, row_at(d, which))

    def pair_at(d):
        return remote(pair_own, pair_in.at[d], pair_s, pair_r, along_y(d))

    slots = (pl.ds(0, 2), pl.ds(2, 3))

    def spread(k, d):
        return same(sums.at[slots[k], rows32(0)], spread_s.at[k], spread_r.at[k], row_at(d))

    def group_at(i):
        return (z + 2 + i // 2) % SIDE * 2 + (y // 2 + 1 + i) % 2

    def load(g):
        return pltpu.make_async_copy(op_hbm.at[pl.ds(4 * g, 4)], op.at[pl.ds(4 * g, 4)], op_sem.at[g])

    partners = (
        [clus_at(z, y, other)]
        + [along_y(d) for d in steps]
        + [along_z(d) for d in steps]
        + [row_at(d, which) for d in steps for which in (core, other)]
    )
    greet(partners)
    omega_in = pltpu.make_async_copy(omega_hbm, omega, in_sem.at[0])
    q_in = pltpu.make_async_copy(q_hbm, q_own, in_sem.at[1])
    near_in_copy = pltpu.make_async_copy(near_hbm, near, in_sem.at[2])
    near_in_copy.start()
    omega_in.start()

    def start_load(i, _):
        load(group_at(i)).start()
        return 0

    lax.fori_loop(0, 8, start_load, 0)
    q_in.start()
    near_in_copy.wait()
    is_near = jnp.max((near[...] == me).astype(F32), axis=0, keepdims=True)
    count = near.shape[1]
    on_row = lax.broadcasted_iota(jnp.int32, (count, count), 0) == lax.broadcasted_iota(jnp.int32, (count, count), 1)
    near_rows = jnp.sum(jnp.where(on_row, jnp.broadcast_to(is_near, (count, count)), 0.0), axis=1, keepdims=True)
    weights[...] = jnp.broadcast_to(1.0 - near_rows, weights.shape)
    omega_in.wait()

    def begin():
        q_in.wait()
        gathered[core, here] = q_own[...].astype(F32).T.astype(BF16)
        pl.semaphore_wait(pltpu.get_barrier_semaphore(), len(partners))
        for d in (2, 1, 3):
            for h in range(2):
                ag1(h, d).start()
        for h in range(2):
            for s in range(2):
                ag2(h, 0, s).start()
        for h in range(2):
            forward(core, h, 0, 0).start()

    def first_in(d):
        for h in range(2):
            ag1(h, d, SIDE - d).wait_recv()
            for s in range(2):
                ag2(h, SIDE - d, s).start()
            forward(core, h, SIDE - d, 0).start()

    def second_in(e):
        for h in range(2):
            for s in range(2):
                ag2(h, e, s, BACK[s]).wait_recv()
                ag2x(h, e, s, BACK[s]).start()
                forward(core, h, e, BACK[s]).start()

    def second_opposite_in(e):
        for h in range(2):
            for s in range(2):
                ag2x(h, e, s, 2).wait_recv()
            forward(core, h, e, 2).start()

    def column(i):
        g = group_at(i)
        load(g).wait()
        product = jnp.dot(
            op[pl.ds(4 * g, 4)].reshape(1024, 1024), omega[...], preferred_element_type=F32
        )
        for j in range(2):
            for which in range(2):
                n = 2 * j + which
                term = (product[256 * n:256 * n + 256] * far(4 * g + n)).astype(BF16)

                @pl.when(core == which)
                def _():
                    own[2 * g + j] = term

                @pl.when(core != which)
                def _():
                    away[2 * g + j] = term


    def column_early(i, _):
        column(i)
        return 0

    def column_late(i, _):
        column(i)
        to_core(group_at(i)).start()
        return 0

    lax.fori_loop(0, EARLY, column_early, 0)
    begin()

    def send_early(i, _):
        to_core(group_at(i)).start()
        return 0

    lax.fori_loop(0, EARLY, send_early, 0)
    lax.fori_loop(EARLY, 8, column_late, 0)

    def pair_sum(i, _):
        g = group_at(i)
        to_core(g).wait_recv()
        for j in range(2):
            at = 2 * g + j
            own[at] = (own[at].astype(F32) + fromcore[at].astype(F32)).astype(BF16)
            zt, yt = at // SIDE, at % SIDE

            @pl.when(zt == (z + 2) % SIDE)
            def _():
                for s in range(2):
                    far_send(0, s, yt).start()

            @pl.when(yt == (y + 2) % SIDE)
            def _():
                for s in range(2):
                    far_send(1, s, zt).start()

        return 0

    lax.fori_loop(0, 8, pair_sum, 0)
    for d in (1, 3, 2):
        first_in(d)
    second_in(0)

    wait_bytes(far_in, far_r)

    def add_far(i, _):
        for h in range(2):
            for s in range(2):
                at = block(h, ahead[s], i)
                own[at, pieces[h][s]] = (own[at, pieces[h][s]].astype(F32) + far_in[h, s, i].astype(F32)).astype(BF16)
                near_send(h, s, i).start()
        return 0

    lax.fori_loop(0, SIDE, add_far, 0)
    for e in (3, 1, 2):
        second_in(e)
    total[...] = jnp.zeros_like(total)

    def scaled(a, b):
        at = spot(0, b, a)
        wait_bytes(gathered.at[other, at], fw_r.at[a, b])
        return jnp.concatenate(
            [(gathered[which, at].astype(F32) * far(2 * at + which)).astype(BF16) for which in range(2)], axis=1
        )

    def row_step(i, _):
        a, b = i // 3 + i // 3 // 2, i % 3 + i % 3 // 2
        both = op[pl.ds(2 * spot(0, b, a), 2)].reshape(512, 1024)
        total[...] += jnp.dot(scaled(a, b), both, preferred_element_type=F32)
        return 0

    lax.fori_loop(0, 9, row_step, 0)
    for e in (0, 3, 1, 2):
        second_opposite_in(e)

    def late_place(i):
        j = i % 4
        return (2 * (1 - i // 4) + i // 4 * (j + j // 2), (1 - i // 4) * i + i // 4 * 2)

    def late_piece(i, _):
        wide[i] = scaled(*late_place(i))
        return 0

    lax.fori_loop(0, 7, late_piece, 0)

    def quarter(d):
        columns = pl.ds(pl.multiple_of((x + d) % SIDE * 256, 256), 256)

        running = total[:, columns]
        for i in range(7):
            a, b = late_place(i)
            both = op[pl.ds(2 * spot(0, b, a), 2), :, columns].reshape(512, 256)
            running = running + jnp.dot(wide[i], both, preferred_element_type=F32)
        return running

    def send_quarter(i, _):
        d = (2 + 3 * i + i // 2 * 3) % SIDE
        vsend[d] = quarter(d).astype(BF16)
        row_send(d).start()
        return 0

    wait_bytes(near_in, near_r)

    def first_sum(i, _):
        for h in range(2):
            part = own[block(h, 0, i), half[h]].astype(F32)
            for s in range(2):
                part = part + near_in[h, s, i].astype(F32)
            parts[h, i] = part.astype(BF16)

            @pl.when(i == (y, z)[h])
            def _():
                u_sum[half[h], :] = part

        return 0

    lax.fori_loop(0, SIDE, first_sum, 0)
    for d in (2, 1, 3):
        for h in range(2):
            last_send(h, d).start()
    lax.fori_loop(0, 3, send_quarter, 0)
    mine = quarter(0)
    for h in range(2):
        wait_bytes(last_in.at[h, pl.ds(1, 3)], last_r.at[h])
        part = u_sum[half[h], :]
        for d in steps:
            part = part + last_in[h, d].astype(F32)
        u_sum[half[h], :] = part
    lead_out[0] = u_sum[:, :R]
    grams[0] = lax.dot_general(
        u_sum[:, :R], u_sum[...], (((0,), (0,)), ((), ())), precision=HIGHEST, preferred_element_type=F32
    )
    for d in (2, 1, 3):
        part_at(d, 0).start()
    wait_bytes(vin.at[pl.ds(1, 3)], v_r)
    for d in steps:
        mine = mine + vin[d].astype(F32)
    lead_out[1] = mine[:R, :].T
    grams[1] = lax.dot_general(
        mine[:R, :], mine, (((1,), (1,)), ((), ())), precision=HIGHEST, preferred_element_type=F32
    )
    for d in (2, 1, 3):
        part_at(d, 1).start()
    part_at(0, other).start()
    part_in[core] = grams[core, rows32(0)]
    wait_bytes(part_in.at[pl.ds(1, 7)], part_r)
    leaf = [part_in[s] + part_in[2 + s] + part_in[4 + s] + part_in[6 + s] for s in range(2)]
    pair = leaf[0] + leaf[1]
    pair_own[...] = pair
    for d in (2, 1, 3):
        pair_at(d).start()
    for s in range(2):
        sums[s, rows32(0)] = leaf[s][:, :R]
    for d in (2, 1, 3):
        spread(0, d).start()
    wait_bytes(pair_in.at[pl.ds(1, 3)], pair_r)
    low, high = y % 2, y // 2
    near_pair = pair_in[3 - 2 * low]
    far_pair = pair_in[2] + pair_in[1 + 2 * low]
    sums[2, rows32(0)] = near_pair[:, :R]
    sums[3, rows32(0)] = far_pair[:, :R]
    sums[4, rows32(0)] = ((pair + near_pair) + far_pair)[:, R:]
    for d in (2, 1, 3):
        spread(1, d).start()
    spread_size = [sums.at[slots[k], pl.ds(0, 96)] for k in range(2)]
    for k in range(2):
        wait_bytes(spread_size[k], spread_r.at[k])

    pair = sums[0] + sums[1]
    quad = pair + sums[2]
    state[0] = sums[0]
    state[1] = sums[1]
    state[2 + low] = pair
    state[3 - low] = sums[2]
    state[4 + high] = quad
    state[5 - high] = sums[3]
    state[6] = quad + sums[3]
    state[7] = sums[4]
    chol_all(state, 7)
    result = remote(state, packed_out.at[core], out_s, out_r, clus_at(z, y, other))
    result.start()
    packed_out[core] = state[...]
    result.wait_recv()

    result.wait_send()
    for ref, sem in (
        (gathered.at[0, pl.ds(0, 3)], ag1_s),
        (gathered.at[0, pl.ds(0, 8)], ag2_s),
        (gathered.at[0, pl.ds(0, 4)], ag2x_s),
        (gathered.at[0], fw_s),
        (away, core_s),
        (far_in, far_s),
        (near_in, near_s),
        (gathered.at[0, pl.ds(0, 3)], last_s),
        (vin.at[pl.ds(1, 3)], v_s),
        (part_in.at[pl.ds(1, 7)], part_s),
        (pair_in.at[pl.ds(1, 3)], pair_s),
        (spread_size[0], spread_s.at[0]),
        (spread_size[1], spread_s.at[1]),
    ):
        wait_bytes(ref, sem)


def grams_of(near_list, operator, omega, omega_rows):
    vmem = pl.BlockSpec(memory_space=pltpu.VMEM)
    sem = pltpu.SemaphoreType.DMA
    block = (256, 256)
    part = (128, 256)

    def buffer(*shape, dtype=BF16):
        return pltpu.VMEM(shape, dtype)

    one = sem(())

    return pl.pallas_call(
        sample_kernel,
        out_shape=[jax.ShapeDtypeStruct((2, 256, R), F32), jax.ShapeDtypeStruct((2, 8, R, R), F32)],
        in_specs=[pl.BlockSpec(memory_space=pltpu.HBM)] * 4,
        out_specs=[vmem, vmem],
        scratch_shapes=[
            buffer(near_list.shape[1], near_list.shape[0], dtype=jnp.int32),
            buffer(operator.shape[0], 256, dtype=F32),
            buffer(*operator.shape),
            buffer(*omega.shape),
            buffer(*block),
            buffer(16, *block),
            buffer(16, *block),
            buffer(16, *block),
            buffer(2, 2, SIDE, 64, 256),
            buffer(2, 2, SIDE, *part),
            buffer(2, SIDE, *part),
            buffer(2, SIDE, *part),
            buffer(2, 16, *block),
            buffer(7, 256, 512),
            buffer(256, 1024, dtype=F32),
            buffer(SIDE, *block),
            buffer(SIDE, *block),
            buffer(*block, dtype=F32),
            buffer(2, R, 256, dtype=F32),
            buffer(8, 32, 256, dtype=F32),
            buffer(32, 256, dtype=F32),
            buffer(SIDE, 32, 256, dtype=F32),
            buffer(5, R, R, dtype=F32),
            buffer(8, R, R, dtype=F32),
            sem((3,)),
            sem((8,)),
            one,
            sem((2, SIDE)),
            one,
            sem((2, SIDE, 2)),
            one,
            sem((2, SIDE, 2)),
            one,
            sem((SIDE, SIDE)),
            one,
            sem((8,)),
            one,
            one,
            one,
            one,
            one,
            sem((2,)),
            one,
            one,
            one,
            one,
            one,
            one,
            sem((2,)),
            sem((2,)),
            one,
            one,
        ],
        compiler_params=pltpu.CompilerParams(
            collective_id=0, has_side_effects=True, vmem_limit_bytes=52 << 20
        ),
        cost_estimate=pl.CostEstimate(flops=1 << 33, bytes_accessed=1 << 24, transcendentals=0),
    )(near_list.T, operator, omega, omega_rows)


def split3(x):
    hi = x.astype(jnp.bfloat16).astype(F32)
    rest = x - hi
    mid = rest.astype(jnp.bfloat16).astype(F32)
    low = rest - mid
    return hi, mid, low


def panel(state, m, first):
    last = first + 8
    rows = state[m, first:last, :]
    place = lax.broadcasted_iota(jnp.int32, (8, R), 0)
    lane = lax.broadcasted_iota(jnp.int32, (8, R), 1)
    cols = [jnp.broadcast_to(rows[:, first + c:first + c + 1], (8, R)) for c in range(8)]
    for c in range(8):
        scale = lax.rsqrt(jnp.broadcast_to(cols[c][c:c + 1, :], (8, R)))
        mult = jnp.where(place > c, cols[c] * scale, 0.0)
        for k in range(c + 1, 8):
            cols[k] = cols[k] - mult * (jnp.broadcast_to(cols[k][c:c + 1, :], (8, R)) * scale)
        pivot = jnp.where(lane == first + c, 1.0, jnp.broadcast_to(rows[c:c + 1, :], (8, R))) * scale
        kept = jnp.where((lane == first + c) & (place > c), 0.0, rows)
        rows = jnp.where(place == c, pivot, kept - mult * pivot)
    state[m, first:last, :] = rows
    if last < R:
        hi, mid, low = split3(rows)
        left = jnp.concatenate([hi, hi, mid, mid, hi, low], axis=0).astype(jnp.bfloat16)
        hi, mid, low = (jnp.where((lane < last) & (lane - first > place), 0.0, part) for part in (hi, mid, low))
        right = jnp.concatenate([hi, mid, hi, mid, low, hi], axis=0).astype(jnp.bfloat16)
        update = lax.dot_general(left, right, (((0,), (0,)), ((), ())), preferred_element_type=F32)
        below = lax.broadcasted_iota(jnp.int32, (R - last, R), 1)
        cleared = jnp.where((below >= first) & (below < last), 0.0, state[m, last:, :])
        state[m, last:, :] = cleared - update[last:, :]


def chol_all(state, count):
    for first in range(0, R, 8):
        for m in range(count):
            panel(state, m, first)


def upper_of(packed):
    row = lax.broadcasted_iota(jnp.int32, (R, R), 0)
    col = lax.broadcasted_iota(jnp.int32, (R, R), 1)
    return jnp.where(col > row, packed, jnp.where(col == row, 1.0 / packed, 0.0))


def inverse_of(packed):
    row = lax.broadcasted_iota(jnp.int32, (R, R), 0)
    col = lax.broadcasted_iota(jnp.int32, (R, R), 1)
    return jnp.where(col <= row, packed, 0.0)


def output_kernel(packed, lead_ref, ub_ref, vb_ref, ut_ref, vt_ref, utop_ref, vtop_ref):
    _, y, core = place_of()
    outer = (((1,), (1,)), ((), ()))
    for s in range(2):
        basis_ref, trans_ref, top_ref = ((ub_ref, ut_ref, utop_ref), (vb_ref, vt_ref, vtop_ref))[s]
        basis_ref[...] = lax.dot_general(
            lead_ref[s], inverse_of(packed[s, core]) * math.sqrt(1024), outer,
            precision=HIGHEST, preferred_element_type=F32,
        )
        for k in range(MERGES):
            inverse = inverse_of(packed[s, (2 + y % 2, 4 + y // 2, 6)[k]]) * math.sqrt(2 * R)
            for h in range(2):
                trans_ref[0, k, h * R:(h + 1) * R, :] = lax.dot_general(
                    upper_of(packed[s, 2 * k + h]), inverse, outer, precision=HIGHEST, preferred_element_type=F32
                )
        top_ref[0, :, :R] = upper_of(packed[s, 6]) * (1.0 / math.sqrt(1024))
        top_ref[0, :, R:] = jnp.dot(
            inverse_of(packed[s, 6]), packed[s, 7], precision=HIGHEST, preferred_element_type=F32
        ) * (1.0 / math.sqrt(1024))


def outputs_of(packed, leading):
    vmem = pl.BlockSpec(memory_space=pltpu.VMEM)
    shapes = [(256, R)] * 2 + [(1, MERGES, 2 * R, R)] * 2 + [(1, R, 2 * R)] * 2
    return pl.pallas_call(
        output_kernel,
        out_shape=[jax.ShapeDtypeStruct(shape, F32) for shape in shapes],
        in_specs=[vmem, vmem],
        out_specs=[vmem] * 6,
        compiler_params=pltpu.CompilerParams(vmem_limit_bytes=40 << 20),
    )(packed, leading)


def body(operator, omega, omega_rows, near_list):
    leading, packed = grams_of(near_list, operator, omega, omega_rows)
    return tuple(outputs_of(packed, leading))


def solution(mesh):
    in_specs = (P(None, "row", "clus"), P("clus", None), P(("clus", "row"), None), P())
    out_specs = (
        P(("clus", "row"), None),
        P(("clus", "row"), None),
        P("clus", None, None, None),
        P("clus", None, None, None),
        P("clus", None, None),
        P("clus", None, None),
    )
    return jax.shard_map(body, mesh=mesh, in_specs=in_specs, out_specs=out_specs, check_vma=False)
```

```python
import math

import jax
import jax.numpy as jnp
from jax import lax
from jax.experimental import pallas as pl
from jax.experimental.pallas import tpu as pltpu
from jax.sharding import PartitionSpec as P

R = 128
F32 = jnp.float32
MERGES = 3


HIGHEST = lax.Precision.HIGHEST


SIDE = 4
MESH = pl.DeviceIdType.MESH
BF16 = jnp.bfloat16
BACK = (3, 1)
EARLY = 2


def place_of():
    clus = lax.axis_index("clus")
    return (clus // 8, clus // 2 % SIDE, clus % 2)


def clus_at(z, y, core):
    return {"clus": (z % SIDE * SIDE + y % SIDE) * 2 + core}


def remote(src, dst, send, recv, device):
    return pltpu.make_async_remote_copy(
        src_ref=src, dst_ref=dst, send_sem=send, recv_sem=recv, device_id=device, device_id_type=MESH
    )


def greet(devices):
    for device in devices:
        pl.semaphore_signal(pltpu.get_barrier_semaphore(), inc=1, device_id=device, device_id_type=MESH)


def sample_kernel(
    near_hbm, op_hbm, omega_hbm, q_hbm, lead_out, packed_out,
    near, weights, op, omega, q_own, own, away, fromcore, far_in, near_in, parts, last_in, gathered, wide, total,
    vsend, vin, u_sum, grams, part_in, pair_own, pair_in, sums, state,
    in_sem, op_sem, ag1_s, ag1_r, ag2_s, ag2_r, ag2x_s, ag2x_r, fw_s, fw_r, core_s, core_r,
    far_s, far_r, near_s, near_r, last_s, last_r, v_s, v_r,
    part_s, part_r, pair_s, pair_r, spread_s, spread_r, out_s, out_r,
):
    z, y, core = place_of()
    x = lax.axis_index("row")
    me = lax.axis_index("clus")
    here = z * SIDE + y
    other = 1 - core
    steps = (1, 2, 3)
    half = (pl.ds(0, 128), pl.ds(128, 128))
    pieces = tuple(tuple(pl.ds(128 * h + 64 * s, 64) for s in range(2)) for h in range(2))
    ahead = (1, 3)

    def far(t):
        return weights[pl.ds(t, 1), :]

    def spot(h, d1, d2):
        dz, dy = (d2, d1) if h == 0 else (d1, d2)
        return (z + dz) % SIDE * SIDE + (y + dy) % SIDE

    def along_y(d):
        return clus_at(z, y + d, core)

    def along_z(d):
        return clus_at(z + d, y, core)

    first = (along_y, along_z)
    second = (along_z, along_y)

    def same(ref, send, recv, device):
        return remote(ref, ref, send, recv, device)

    def ag1(h, d, d1=0):
        return same(gathered.at[core, spot(h, d1, 0), half[h]], ag1_s, ag1_r.at[h, d], first[h](d))

    def ag2(h, e, s, d2=0):
        return same(gathered.at[core, spot(h, e, d2), half[h]], ag2_s, ag2_r.at[h, e, s], second[h](ahead[s]))

    def ag2x(h, e, s, d2):
        return same(gathered.at[core, spot(h, e, d2), pieces[h][s]], ag2x_s, ag2x_r.at[h, e, s], second[h](ahead[s]))

    def forward(which, h, d1, d2):
        a, b = (d2, d1) if h == 0 else (d1, d2)
        return same(gathered.at[which, spot(h, d1, d2), half[h]], fw_s, fw_r.at[a, b], clus_at(z, y, other))

    def to_core(g):
        two = pl.ds(2 * g, 2)
        return remote(away.at[two], fromcore.at[two], core_s, core_r.at[g], clus_at(z, y, other))

    def wait_bytes(ref, sem):
        pltpu.make_async_copy(ref, ref, sem).wait()

    def block(h, d, i):
        return (z + d) % SIDE * SIDE + i if h == 0 else i * SIDE + (y + d) % SIDE

    def far_send(h, s, i):
        return remote(own.at[block(h, 2, i), pieces[h][s]], far_in.at[h, s, i], far_s, far_r, second[h](ahead[s]))

    def near_send(h, s, i):
        return remote(own.at[block(h, ahead[s], i), half[h]], near_in.at[h, s, i], near_s, near_r, second[h](ahead[s]))

    def last_send(h, d):
        i = ((y if h == 0 else z) + d) % SIDE
        return remote(parts.at[h, i], last_in.at[h, d], last_s, last_r.at[h], first[h](d))

    def row_at(d, which=None):
        xt = (x + d) % SIDE
        return {"row": xt} if which is None else {"row": xt, "clus": here * 2 + which}

    def row_send(d):
        return remote(vsend.at[d], vin.at[d], v_s, v_r, row_at(d))

    def rows32(d):
        return pl.ds(pl.multiple_of((x + d) % SIDE * 32, 32), 32)

    def part_at(d, which):
        return remote(grams.at[which, rows32(d)], part_in.at[2 * d + core], part_s, part_r, row_at(d, which))

    def pair_at(d):
        return remote(pair_own, pair_in.at[d], pair_s, pair_r, along_y(d))

    slots = (pl.ds(0, 2), pl.ds(2, 3))

    def spread(k, d):
        return same(sums.at[slots[k], rows32(0)], spread_s.at[k], spread_r.at[k], row_at(d))

    def group_at(i):
        return (z + 2 + i // 2) % SIDE * 2 + (y // 2 + 1 + i) % 2

    def load(g):
        return pltpu.make_async_copy(op_hbm.at[pl.ds(4 * g, 4)], op.at[pl.ds(4 * g, 4)], op_sem.at[g])

    partners = (
        [clus_at(z, y, other)]
        + [along_y(d) for d in steps]
        + [along_z(d) for d in steps]
        + [row_at(d, which) for d in steps for which in (core, other)]
    )
    greet(partners)
    omega_in = pltpu.make_async_copy(omega_hbm, omega, in_sem.at[0])
    q_in = pltpu.make_async_copy(q_hbm, q_own, in_sem.at[1])
    near_in_copy = pltpu.make_async_copy(near_hbm, near, in_sem.at[2])
    near_in_copy.start()
    omega_in.start()

    def start_load(i, _):
        load(group_at(i)).start()
        return 0

    lax.fori_loop(0, 8, start_load, 0)
    q_in.start()
    near_in_copy.wait()
    is_near = jnp.max((near[...] == me).astype(F32), axis=0, keepdims=True)
    count = near.shape[1]
    on_row = lax.broadcasted_iota(jnp.int32, (count, count), 0) == lax.broadcasted_iota(jnp.int32, (count, count), 1)
    near_rows = jnp.sum(jnp.where(on_row, jnp.broadcast_to(is_near, (count, count)), 0.0), axis=1, keepdims=True)
    weights[...] = jnp.broadcast_to(1.0 - near_rows, weights.shape)
    omega_in.wait()

    def begin():
        q_in.wait()
        gathered[core, here] = q_own[...].astype(F32).T.astype(BF16)
        pl.semaphore_wait(pltpu.get_barrier_semaphore(), len(partners))
        for d in (2, 1, 3):
            for h in range(2):
                ag1(h, d).start()
        for h in range(2):
            for s in range(2):
                ag2(h, 0, s).start()
        for h in range(2):
            forward(core, h, 0, 0).start()

    def first_in(d):
        for h in range(2):
            ag1(h, d, SIDE - d).wait_recv()
            for s in range(2):
                ag2(h, SIDE - d, s).start()
            forward(core, h, SIDE - d, 0).start()

    def second_in(e):
        for h in range(2):
            for s in range(2):
                ag2(h, e, s, BACK[s]).wait_recv()
                ag2x(h, e, s, BACK[s]).start()
                forward(core, h, e, BACK[s]).start()

    def second_opposite_in(e):
        for h in range(2):
            for s in range(2):
                ag2x(h, e, s, 2).wait_recv()
            forward(core, h, e, 2).start()

    def column(i):
        g = group_at(i)
        load(g).wait()
        product = jnp.dot(
            op[pl.ds(4 * g, 4)].reshape(1024, 1024), omega[...], preferred_element_type=F32
        )
        for j in range(2):
            for which in range(2):
                n = 2 * j + which
                term = (product[256 * n:256 * n + 256] * far(4 * g + n)).astype(BF16)

                @pl.when(core == which)
                def _():
                    own[2 * g + j] = term

                @pl.when(core != which)
                def _():
                    away[2 * g + j] = term


    def column_early(i, _):
        column(i)
        return 0

    def column_late(i, _):
        column(i)
        to_core(group_at(i)).start()
        return 0

    lax.fori_loop(0, EARLY, column_early, 0)
    begin()

    def send_early(i, _):
        to_core(group_at(i)).start()
        return 0

    lax.fori_loop(0, EARLY, send_early, 0)
    lax.fori_loop(EARLY, 6, column_late, 0)
    for d in (1, 3, 2):
        first_in(d)
    lax.fori_loop(6, 8, column_late, 0)

    def pair_sum(i, _):
        g = group_at(i)
        to_core(g).wait_recv()
        for j in range(2):
            at = 2 * g + j
            own[at] = (own[at].astype(F32) + fromcore[at].astype(F32)).astype(BF16)
            zt, yt = at // SIDE, at % SIDE

            @pl.when(zt == (z + 2) % SIDE)
            def _():
                for s in range(2):
                    far_send(0, s, yt).start()

            @pl.when(yt == (y + 2) % SIDE)
            def _():
                for s in range(2):
                    far_send(1, s, zt).start()

        return 0

    lax.fori_loop(0, 8, pair_sum, 0)
    second_in(0)
    total[...] = jnp.zeros_like(total)

    def scaled(a, b):
        at = spot(0, b, a)
        wait_bytes(gathered.at[other, at], fw_r.at[a, b])
        return jnp.concatenate(
            [(gathered[which, at].astype(F32) * far(2 * at + which)).astype(BF16) for which in range(2)], axis=1
        )

    def row_step(a, b):
        both = op[pl.ds(2 * spot(0, b, a), 2)].reshape(512, 1024)
        total[...] += jnp.dot(scaled(a, b), both, preferred_element_type=F32)
        return 0

    lax.fori_loop(0, 3, lambda i, _: row_step(0, i + i // 2), 0)
    lax.fori_loop(0, 2, lambda i, _: row_step(1 + 2 * i, 0), 0)
    second_in(3)
    second_in(1)
    second_in(2)

    wait_bytes(far_in, far_r)

    def add_far(i, _):
        for h in range(2):
            for s in range(2):
                at = block(h, ahead[s], i)
                own[at, pieces[h][s]] = (own[at, pieces[h][s]].astype(F32) + far_in[h, s, i].astype(F32)).astype(BF16)
                near_send(h, s, i).start()
        return 0

    lax.fori_loop(0, SIDE, add_far, 0)
    lax.fori_loop(0, 4, lambda i, _: row_step(1 + i // 2 * 2, 1 + i % 2 * 2), 0)
    for e in (0, 3, 1, 2):
        second_opposite_in(e)

    def late_place(i):
        j = i % 4
        return (2 * (1 - i // 4) + i // 4 * (j + j // 2), (1 - i // 4) * i + i // 4 * 2)

    def late_piece(i, _):
        wide[i] = scaled(*late_place(i))
        return 0

    lax.fori_loop(0, 7, late_piece, 0)

    def quarter(d):
        columns = pl.ds(pl.multiple_of((x + d) % SIDE * 256, 256), 256)

        running = total[:, columns]
        for i in range(7):
            a, b = late_place(i)
            both = op[pl.ds(2 * spot(0, b, a), 2), :, columns].reshape(512, 256)
            running = running + jnp.dot(wide[i], both, preferred_element_type=F32)
        return running

    def send_quarter(i, _):
        d = (2 + 3 * i + i // 2 * 3) % SIDE
        vsend[d] = quarter(d).astype(BF16)
        row_send(d).start()
        return 0

    lax.fori_loop(0, 3, send_quarter, 0)

    wait_bytes(near_in, near_r)

    def first_sum(i, _):
        for h in range(2):
            part = own[block(h, 0, i), half[h]].astype(F32)
            for s in range(2):
                part = part + near_in[h, s, i].astype(F32)
            parts[h, i] = part.astype(BF16)

            @pl.when(i == (y, z)[h])
            def _():
                u_sum[half[h], :] = part

        return 0

    lax.fori_loop(0, SIDE, first_sum, 0)
    for d in (2, 1, 3):
        for h in range(2):
            last_send(h, d).start()
    mine = quarter(0)
    for h in range(2):
        wait_bytes(last_in.at[h, pl.ds(1, 3)], last_r.at[h])
        part = u_sum[half[h], :]
        for d in steps:
            part = part + last_in[h, d].astype(F32)
        u_sum[half[h], :] = part
    lead_out[0] = u_sum[:, :R]
    grams[0] = lax.dot_general(
        u_sum[:, :R], u_sum[...], (((0,), (0,)), ((), ())), precision=HIGHEST, preferred_element_type=F32
    )
    for d in (2, 1, 3):
        part_at(d, 0).start()
    wait_bytes(vin.at[pl.ds(1, 3)], v_r)
    for d in steps:
        mine = mine + vin[d].astype(F32)
    lead_out[1] = mine[:R, :].T
    grams[1] = lax.dot_general(
        mine[:R, :], mine, (((1,), (1,)), ((), ())), precision=HIGHEST, preferred_element_type=F32
    )
    for d in (2, 1, 3):
        part_at(d, 1).start()
    part_at(0, other).start()
    part_in[core] = grams[core, rows32(0)]
    wait_bytes(part_in.at[pl.ds(1, 7)], part_r)
    leaf = [part_in[s] + part_in[2 + s] + part_in[4 + s] + part_in[6 + s] for s in range(2)]
    pair = leaf[0] + leaf[1]
    pair_own[...] = pair
    for d in (2, 1, 3):
        pair_at(d).start()
    for s in range(2):
        sums[s, rows32(0)] = leaf[s][:, :R]
    for d in (2, 1, 3):
        spread(0, d).start()
    wait_bytes(pair_in.at[pl.ds(1, 3)], pair_r)
    low, high = y % 2, y // 2
    near_pair = pair_in[3 - 2 * low]
    far_pair = pair_in[2] + pair_in[1 + 2 * low]
    sums[2, rows32(0)] = near_pair[:, :R]
    sums[3, rows32(0)] = far_pair[:, :R]
    sums[4, rows32(0)] = ((pair + near_pair) + far_pair)[:, R:]
    for d in (2, 1, 3):
        spread(1, d).start()
    spread_size = [sums.at[slots[k], pl.ds(0, 96)] for k in range(2)]
    for k in range(2):
        wait_bytes(spread_size[k], spread_r.at[k])

    pair = sums[0] + sums[1]
    quad = pair + sums[2]
    state[0] = sums[0]
    state[1] = sums[1]
    state[2 + low] = pair
    state[3 - low] = sums[2]
    state[4 + high] = quad
    state[5 - high] = sums[3]
    state[6] = quad + sums[3]
    state[7] = sums[4]
    chol_all(state, 7)
    result = remote(state, packed_out.at[core], out_s, out_r, clus_at(z, y, other))
    result.start()
    packed_out[core] = state[...]
    result.wait_recv()

    result.wait_send()
    for ref, sem in (
        (gathered.at[0, pl.ds(0, 3)], ag1_s),
        (gathered.at[0, pl.ds(0, 8)], ag2_s),
        (gathered.at[0, pl.ds(0, 4)], ag2x_s),
        (gathered.at[0], fw_s),
        (away, core_s),
        (far_in, far_s),
        (near_in, near_s),
        (gathered.at[0, pl.ds(0, 3)], last_s),
        (vin.at[pl.ds(1, 3)], v_s),
        (part_in.at[pl.ds(1, 7)], part_s),
        (pair_in.at[pl.ds(1, 3)], pair_s),
        (spread_size[0], spread_s.at[0]),
        (spread_size[1], spread_s.at[1]),
    ):
        wait_bytes(ref, sem)


def grams_of(near_list, operator, omega, omega_rows):
    vmem = pl.BlockSpec(memory_space=pltpu.VMEM)
    sem = pltpu.SemaphoreType.DMA
    block = (256, 256)
    part = (128, 256)

    def buffer(*shape, dtype=BF16):
        return pltpu.VMEM(shape, dtype)

    one = sem(())

    return pl.pallas_call(
        sample_kernel,
        out_shape=[jax.ShapeDtypeStruct((2, 256, R), F32), jax.ShapeDtypeStruct((2, 8, R, R), F32)],
        in_specs=[pl.BlockSpec(memory_space=pltpu.HBM)] * 4,
        out_specs=[vmem, vmem],
        scratch_shapes=[
            buffer(near_list.shape[1], near_list.shape[0], dtype=jnp.int32),
            buffer(operator.shape[0], 256, dtype=F32),
            buffer(*operator.shape),
            buffer(*omega.shape),
            buffer(*block),
            buffer(16, *block),
            buffer(16, *block),
            buffer(16, *block),
            buffer(2, 2, SIDE, 64, 256),
            buffer(2, 2, SIDE, *part),
            buffer(2, SIDE, *part),
            buffer(2, SIDE, *part),
            buffer(2, 16, *block),
            buffer(7, 256, 512),
            buffer(256, 1024, dtype=F32),
            buffer(SIDE, *block),
            buffer(SIDE, *block),
            buffer(*block, dtype=F32),
            buffer(2, R, 256, dtype=F32),
            buffer(8, 32, 256, dtype=F32),
            buffer(32, 256, dtype=F32),
            buffer(SIDE, 32, 256, dtype=F32),
            buffer(5, R, R, dtype=F32),
            buffer(8, R, R, dtype=F32),
            sem((3,)),
            sem((8,)),
            one,
            sem((2, SIDE)),
            one,
            sem((2, SIDE, 2)),
            one,
            sem((2, SIDE, 2)),
            one,
            sem((SIDE, SIDE)),
            one,
            sem((8,)),
            one,
            one,
            one,
            one,
            one,
            sem((2,)),
            one,
            one,
            one,
            one,
            one,
            one,
            sem((2,)),
            sem((2,)),
            one,
            one,
        ],
        compiler_params=pltpu.CompilerParams(
            collective_id=0, has_side_effects=True, vmem_limit_bytes=52 << 20
        ),
        cost_estimate=pl.CostEstimate(flops=1 << 33, bytes_accessed=1 << 24, transcendentals=0),
    )(near_list.T, operator, omega, omega_rows)


def split3(x):
    hi = x.astype(jnp.bfloat16).astype(F32)
    rest = x - hi
    mid = rest.astype(jnp.bfloat16).astype(F32)
    low = rest - mid
    return hi, mid, low


def panel(state, m, first):
    last = first + 8
    rows = state[m, first:last, :]
    place = lax.broadcasted_iota(jnp.int32, (8, R), 0)
    lane = lax.broadcasted_iota(jnp.int32, (8, R), 1)
    cols = [jnp.broadcast_to(rows[:, first + c:first + c + 1], (8, R)) for c in range(8)]
    for c in range(8):
        scale = lax.rsqrt(jnp.broadcast_to(cols[c][c:c + 1, :], (8, R)))
        mult = jnp.where(place > c, cols[c] * (scale * scale), 0.0)
        for k in range(c + 1, 8):
            cols[k] = cols[k] - mult * jnp.broadcast_to(cols[k][c:c + 1, :], (8, R))
        pivot = jnp.where(lane == first + c, 1.0, jnp.broadcast_to(rows[c:c + 1, :], (8, R)))
        kept = jnp.where((lane == first + c) & (place > c), 0.0, rows)
        rows = jnp.where(place == c, pivot * scale, kept - mult * pivot)
    state[m, first:last, :] = rows
    if last < R:
        hi, mid, low = split3(rows)
        left = jnp.concatenate([hi, hi, mid, mid, hi, low], axis=0).astype(jnp.bfloat16)
        hi, mid, low = (jnp.where((lane < last) & (lane - first > place), 0.0, part) for part in (hi, mid, low))
        right = jnp.concatenate([hi, mid, hi, mid, low, hi], axis=0).astype(jnp.bfloat16)
        update = lax.dot_general(left, right, (((0,), (0,)), ((), ())), preferred_element_type=F32)
        below = lax.broadcasted_iota(jnp.int32, (R - last, R), 1)
        cleared = jnp.where((below >= first) & (below < last), 0.0, state[m, last:, :])
        state[m, last:, :] = cleared - update[last:, :]


def chol_all(state, count):
    for first in range(0, R, 8):
        for m in range(count):
            panel(state, m, first)


def upper_of(packed):
    row = lax.broadcasted_iota(jnp.int32, (R, R), 0)
    col = lax.broadcasted_iota(jnp.int32, (R, R), 1)
    return jnp.where(col > row, packed, jnp.where(col == row, 1.0 / packed, 0.0))


def inverse_of(packed):
    row = lax.broadcasted_iota(jnp.int32, (R, R), 0)
    col = lax.broadcasted_iota(jnp.int32, (R, R), 1)
    return jnp.where(col <= row, packed, 0.0)


def output_kernel(packed, lead_ref, ub_ref, vb_ref, ut_ref, vt_ref, utop_ref, vtop_ref):
    _, y, core = place_of()
    outer = (((1,), (1,)), ((), ()))
    for s in range(2):
        basis_ref, trans_ref, top_ref = ((ub_ref, ut_ref, utop_ref), (vb_ref, vt_ref, vtop_ref))[s]
        basis_ref[...] = lax.dot_general(
            lead_ref[s], inverse_of(packed[s, core]) * math.sqrt(1024), outer,
            precision=HIGHEST, preferred_element_type=F32,
        )
        for k in range(MERGES):
            inverse = inverse_of(packed[s, (2 + y % 2, 4 + y // 2, 6)[k]]) * math.sqrt(2 * R)
            for h in range(2):
                trans_ref[0, k, h * R:(h + 1) * R, :] = lax.dot_general(
                    upper_of(packed[s, 2 * k + h]), inverse, outer, precision=HIGHEST, preferred_element_type=F32
                )
        top_ref[0, :, :R] = upper_of(packed[s, 6]) * (1.0 / math.sqrt(1024))
        top_ref[0, :, R:] = jnp.dot(
            inverse_of(packed[s, 6]), packed[s, 7], precision=HIGHEST, preferred_element_type=F32
        ) * (1.0 / math.sqrt(1024))


def outputs_of(packed, leading):
    vmem = pl.BlockSpec(memory_space=pltpu.VMEM)
    shapes = [(256, R)] * 2 + [(1, MERGES, 2 * R, R)] * 2 + [(1, R, 2 * R)] * 2
    return pl.pallas_call(
        output_kernel,
        out_shape=[jax.ShapeDtypeStruct(shape, F32) for shape in shapes],
        in_specs=[vmem, vmem],
        out_specs=[vmem] * 6,
        compiler_params=pltpu.CompilerParams(vmem_limit_bytes=40 << 20),
    )(packed, leading)


def body(operator, omega, omega_rows, near_list):
    leading, packed = grams_of(near_list, operator, omega, omega_rows)
    return tuple(outputs_of(packed, leading))


def solution(mesh):
    in_specs = (P(None, "row", "clus"), P("clus", None), P(("clus", "row"), None), P())
    out_specs = (
        P(("clus", "row"), None),
        P(("clus", "row"), None),
        P("clus", None, None, None),
        P("clus", None, None, None),
        P("clus", None, None),
        P("clus", None, None),
    )
    return jax.shard_map(body, mesh=mesh, in_specs=in_specs, out_specs=out_specs, check_vma=False)
```
